512 devices in a mesh: row: 4 (over x), rad: 16 (over z), ax: 8 (over y, core).
Axes of the slice: x: 4, y: 4, z: 16, core: 2. Of those that a mesh axis runs over, the one named last changes fastest.
Arguments:
- state: float32 [7, 4, 128, 64, 128], P(None, 'row', 'rad', 'ax'), may hold values from -6 to 6
- axial_speed: float32 [4, 128, 64, 128], P('row', 'rad', 'ax'), may hold values from 0.3 to 1
- viscosity: float32 [4, 128, 64, 128], P('row', 'rad', 'ax'), may hold values from 0.02 to 0.1
- relaxation: float32 [7], replicated, may hold values from 0.05 to 0.5
- face_area: float32 [4, 128, 64], P('row', 'rad', 'ax'), may hold values from 1 to 10
- face_station: int32 [4, 128, 64], P('row', 'rad', 'ax'), may hold values from 0 to 127, as said below
- limiter_flags: int32 [4, 128, 64], P('row', 'rad', 'ax'), may hold values 0 or 1
- inlet_profile: float32 [7, 128], P(None, 'rad'), may hold values from -6 to 6
Outputs:
- new_state: float32 [7, 4, 128, 64, 128], P(None, 'row', 'rad', 'ax')
- outlet_profile: float32 [7, 4, 128], P(None, 'row', 'rad')
- outlet_pressure: float32 [4, 128], P('row', 'rad')
The draws below stay inside these ranges and needn't reach their ends.
Inputs may be any that keep to these rules, and one draw needn't show every extreme that they name: `face_station`: a face cell at radial index i has a station in the aligned group of 8 stations that holds i, and at circumferential index 0 its station is i itself.
All inputs are finite; a program needn't handle non-finite values. No bound on the sum of `limiter_flags` on one device may be relied on, other than what follows from the above.
Results may differ from the reference program's by a relative error of at most 0.0003.
Values sent between devices are 32-bit elements; how exact they have to be, the bound alone decides.
A program may use at most 64 MiB of HBM per device.

```python
import math
import jax
import jax.numpy as jnp

NV = 7
RC = 8
NX = 128
SWEEPS = 4
ROWS = 4
NR = 128
NC = 64
STATIONS = 128


def draw_face_station(key, part):
    key = jax.random.fold_in(key, 11)
    radial = jnp.arange(NR, dtype=jnp.int32)[None, :, None]
    pitch = jnp.arange(NC, dtype=jnp.int32)[None, None, :]
    offsets = jax.random.randint(key, (ROWS, NR, NC), 0, RC, dtype=jnp.int32)
    grouped = radial // RC * RC + offsets
    return jnp.where(pitch == 0, radial + 0 * offsets, grouped).astype(jnp.int32)


def touch_ends(entries, rng, smallest, high):
    shape = entries.shape
    place = [jax.random.randint(jax.random.fold_in(rng, axis), (), 0, shape[axis]) for axis in range(len(shape))]
    entries = entries.at[tuple(place)].set(smallest)
    longest = shape.index(max(shape))
    place[longest] = (place[longest] + 1) % shape[longest]
    return entries.at[tuple(place)].set(high)


def block_levels(rng, dims, split, smallest, largest):
    def one(position, blocks):
        draws = jax.random.uniform(jax.random.fold_in(jax.random.fold_in(rng, 6), position), (blocks,), jnp.float32, smallest / len(split), largest / len(split))
        return jnp.repeat(jnp.exp(draws), dims[position] // blocks).reshape((-1,) + (1,) * (len(dims) - position - 1))

    gain = one(*split[0])
    for cut in split[1:]:
        gain = gain * one(*cut)
    return gain


def centred(own_key, extent, scale, bound, cuts=(), kind=jnp.bfloat16):
    values = scale * jax.random.normal(own_key, extent, jnp.float32)
    if cuts:
        values = values * block_levels(own_key, extent, cuts, -0.22, 0.18)
    return jnp.clip(values, -bound, bound).astype(kind)


def setup_inputs(seed: int = 0) -> dict:
    key_of = jax.random.split(jax.random.key(seed), 9)
    return {
        "state": centred(key_of[0], (NV, ROWS, NR, NC, NX), 1.0, 6.0, ((1, 4), (2, 16), (3, 8)), jnp.float32),
        "axial_speed": jnp.clip(0.3 + 0.7 * jax.random.uniform(key_of[1], (ROWS, NR, NC, NX), jnp.float32) ** block_levels(key_of[1], (ROWS, NR, NC, NX), ((0, 4), (1, 16), (2, 8)), -0.2, 0.2), 0.3, 1.0),
        "viscosity": jnp.clip(jnp.exp(math.log(0.1) - 1.609438 * jax.random.uniform(key_of[2], (ROWS, NR, NC, NX), jnp.float32) ** block_levels(key_of[2], (ROWS, NR, NC, NX), ((0, 4), (1, 16), (2, 8)), -0.2, 0.2)), 0.02, 0.1),
        "relaxation": jnp.clip(jnp.exp(jax.random.uniform(key_of[3], (NV,), jnp.float32, math.log(0.05), math.log(0.5))), 0.05, 0.5),
        "face_area": jnp.clip(jnp.exp(math.log(10.0) - 2.3025851 * jax.random.uniform(key_of[4], (ROWS, NR, NC), jnp.float32) ** block_levels(key_of[4], (ROWS, NR, NC), ((0, 4), (1, 16), (2, 8)), -0.2, 0.2)), 1.0, 10.0),
        "face_station": draw_face_station(jax.random.fold_in(key_of[8], 71), 0),
        "limiter_flags": touch_ends((jax.random.randint(key_of[6], (ROWS, NR, NC), 0, 2) < 1).astype(jnp.int32), jax.random.fold_in(key_of[6], 1), 0, 1),
        "inlet_profile": centred(key_of[7], (NV, STATIONS), 1.0, 6.0, ((1, 16),), jnp.float32),
    }


pseudo_step = 0.5


def limited_slope(first, second):
    return 0.5 * (jnp.sign(first) + jnp.sign(second)) * jnp.minimum(jnp.abs(first), jnp.abs(second))


def advance(field, inlet_ghost, outlet_ghost, radial_plus, radial_minus, pitch_plus, pitch_minus, axial_speed, viscosity, relax_column, flags):
    length = field.shape[-1]
    extended = jnp.concatenate([inlet_ghost[..., None], inlet_ghost[..., None], field, outlet_ghost[..., None]], axis=-1)
    upwind_two = extended[..., 0:length + 1]
    upwind_one = extended[..., 1:length + 2]
    downwind = extended[..., 2:length + 3]
    face_speed = jnp.concatenate([axial_speed[..., :1], axial_speed], axis=-1)
    left_state = upwind_one + 0.5 * flags[..., None] * limited_slope(upwind_one - upwind_two, downwind - upwind_one)
    face_flux = face_speed * left_state
    convection = face_flux[..., :-1] - face_flux[..., 1:]
    laplacian = extended[..., 3:length + 3] + extended[..., 1:length + 1] + radial_plus + radial_minus + pitch_plus + pitch_minus - 6.0 * field
    return field + pseudo_step * (convection + viscosity * laplacian - relax_column * field)


def reference(state, axial_speed, viscosity, relaxation, face_area, face_station, limiter_flags, inlet_profile):
    field = state
    flags = limiter_flags.astype(jnp.float32)
    relax_column = relaxation[:, None, None, None, None]
    segment_ids = (face_station + STATIONS * jnp.arange(ROWS, dtype=jnp.int32)[:, None, None]).reshape(-1)
    station_index = face_station.reshape(ROWS, -1)
    station_radius = 1.0 + jnp.arange(STATIONS, dtype=jnp.float32) / STATIONS
    profile = None
    pressure = None
    for sweep_index in range(SWEEPS):
        outlet_cells = field[..., -1]
        weighted = (face_area[None] * outlet_cells).reshape(NV, -1).T
        numerator = jax.ops.segment_sum(weighted, segment_ids, ROWS * STATIONS).T.reshape(NV, ROWS, STATIONS)
        denominator = jax.ops.segment_sum(face_area.reshape(-1), segment_ids, ROWS * STATIONS).reshape(ROWS, STATIONS)
        profile = numerator / denominator[None]
        swirl_term = profile[3] * profile[3] / station_radius[None]
        pressure = profile[4] + (4.0 / STATIONS) * (jnp.cumsum(swirl_term, axis=-1) - swirl_term)
        upstream = jnp.concatenate([inlet_profile[:, None], profile[:, :-1]], axis=1)
        index_all = jnp.broadcast_to(station_index[None], (NV, ROWS, NR * NC))
        inlet_ghost = jnp.take_along_axis(upstream, index_all, axis=2).reshape(NV, ROWS, NR, NC)
        pressure_cells = jnp.take_along_axis(pressure, station_index, axis=1).reshape(ROWS, NR, NC)
        outlet_ghost = jnp.concatenate([outlet_cells[:4], pressure_cells[None], outlet_cells[5:]], axis=0)
        padded = jnp.pad(field, ((0, 0), (0, 0), (1, 1), (0, 0), (0, 0)))
        field = advance(field, inlet_ghost, outlet_ghost, padded[:, :, 2:], padded[:, :, :-2],
                        jnp.roll(field, -1, axis=3), jnp.roll(field, 1, axis=3),
                        axial_speed, viscosity, relax_column, flags)
    return field, profile, pressure
```

```python
import functools

import jax
import jax.numpy as jnp
from jax import lax
from jax.experimental import pallas as pl
from jax.experimental.pallas import tpu as pltpu
from jax.sharding import PartitionSpec as P

MESH = pl.DeviceIdType.MESH
SWEEPS = 4
NV = 7
PV = 4
SV = 3
RC = 8
CC = 8
NX = 128
REACH = 4


def kernel(
    sizes,
    state,
    speed,
    visc,
    relax,
    area,
    station,
    flags,
    inlet,
    out,
    out_profile,
    out_pressure,
    field,
    axs,
    axr,
    radr,
    ms_src,
    ms_own,
    ms_up,
    t_src,
    px,
    coef,
    weight,
    hot,
    upstream,
    inlet_t,
    ghosts,
    profile_s,
    s_ax,
    r_ax,
    s_rad,
    r_rad,
    s_own,
    r_own,
    s_down,
    r_up,
    s_px,
    r_px,
    ready,
):
    rows, rads, axes = sizes
    row, rad, ax = lax.axis_index("row"), lax.axis_index("rad"), lax.axis_index("ax")
    lane = lax.broadcasted_iota(jnp.int32, (8, NX), 1)
    sub = lax.broadcasted_iota(jnp.int32, (8, NX), 0)
    zero = jnp.zeros((8, NX), jnp.float32)

    def remote(src, dst, ssem, rsem, where):
        return pltpu.make_async_remote_copy(
            src_ref=src, dst_ref=dst, send_sem=ssem, recv_sem=rsem, device_id=where, device_id_type=MESH
        )

    barrier = pltpu.get_barrier_semaphore()

    def greet(where):
        pl.semaphore_signal(barrier, inc=1, device_id=where, device_id_type=MESH)

    for d in range(1, axes):
        greet({"ax": lax.rem(ax + d, axes)})

    @pl.when(rad > 0)
    def _():
        greet({"rad": rad - 1})

    for d in range(1, REACH + 1):

        @pl.when(rad + d < rads)
        def _():
            greet({"rad": rad + d})

    @pl.when(row > 0)
    def _():
        for d in range(axes):
            greet({"row": row - 1, "ax": d})

    @pl.when(rad == 0)
    def _():
        radr[:, 0] = jnp.zeros_like(radr[:, 0])

    @pl.when(rad == rads - 1)
    def _():
        radr[:, 1] = jnp.zeros_like(radr[:, 1])

    for d in range(1, REACH + 1):

        @pl.when(rad < d)
        def _():
            px[:, d - 1] = jnp.zeros_like(px[:, d - 1])

    diagonal = sub == lane

    def column(ref, r):
        wide = jnp.broadcast_to(ref[r : r + 1, :], (8, 8))
        return jnp.sum(jnp.where(diagonal[:, :8], wide, 0.0), axis=1, keepdims=True)

    areas = area[...]
    local_station = (station[...] - rad * RC).astype(jnp.float32)
    flag = flags[...].astype(jnp.float32)
    for r in range(RC):
        st = jnp.broadcast_to(column(local_station, r), (8, NX))
        ar = jnp.broadcast_to(column(areas, r), (8, NX))
        hot[r] = st
        for s in range(RC):
            weight[s, r] = jnp.where(st == float(s), ar, 0.0)
        a = 0.5 * speed[r]
        coef[0, r] = a
        coef[1, r] = a * (0.5 * jnp.broadcast_to(column(flag, r), (8, NX)))
        coef[2, r] = 0.5 * visc[r]
    turned = zero
    inlet_all = inlet[...]
    for v in range(NV):
        turned = jnp.where(lane == v, column(inlet_all, v), turned)
    inlet_t[...] = turned

    def sums(picks, p):
        total = zero
        for s in range(RC):
            acc = weight[s, 0] * picks[0]
            for r in range(1, RC):
                acc = acc + weight[s, r] * picks[r]
            total = jnp.where(sub == s, jnp.sum(acc, axis=0, keepdims=True), total)
        ms_src[p] = total
        ms_own[p, ax] = total

    def pack(src, p, v):
        for r in range(RC):
            axs[p, 0, v, r : r + 1, :] = src[v, r, 0:1, :]
            axs[p, 1, v, r : r + 1, :] = src[v, r, CC - 1 : CC, :]

    def tail(x):
        return jnp.broadcast_to(x[:, NX - 1 : NX], (8, NX))

    def first(v, picks):
        pack(state, 0, v)
        return tuple(jnp.where(lane == v, tail(state[v, r]), picks[r]) for r in range(RC))

    one = jnp.where(lane == NV, 1.0, 0.0)
    picks = lax.fori_loop(0, NV, first, (one,) * RC)
    sums(picks, 0)

    count = (axes - 1) + jnp.where(rad < rads - 1, 1, 0) + jnp.where(row < rows - 1, axes, 0)
    for d in range(1, REACH + 1):
        count = count + jnp.where(rad >= d, 1, 0)
    pl.semaphore_wait(barrier, count)
    for d in range(2, REACH + 1):

        @pl.when(rad >= d)
        def _():
            pl.semaphore_signal(ready, inc=1, device_id={"rad": rad - d}, device_id_type=MESH)

    last = SWEEPS

    def of(p):
        return state if p == 0 else field.at[p - 1]

    def rad_copy(p, up):
        src = of(p)
        edge = RC - 1 if up else 0
        where = {"rad": rad + 1 if up else rad - 1}
        side = 0 if up else 1
        if p == last:
            return remote(src.at[PV, edge], radr.at[p, side, PV], s_rad.at[p, side], r_rad.at[p, side], where)
        return remote(src.at[:, edge], radr.at[p, side], s_rad.at[p, side], r_rad.at[p, side], where)

    def ax_copy(p, up):
        cell = 1 if up else 0
        where = {"ax": lax.rem(ax + (1 if up else axes - 1), axes)}
        side = 0 if up else 1
        if p == last:
            return remote(axs.at[p, cell, PV], axr.at[p, side, PV], s_ax.at[p, side], r_ax.at[p, side], where)
        return remote(axs.at[p, cell], axr.at[p, side], s_ax.at[p, side], r_ax.at[p, side], where)

    def total_copy(p, d):
        slot = 0 if d < REACH else 1
        return remote(t_src.at[p, slot], px.at[p, d - 1], s_px.at[p, d - 1], r_px.at[p, d - 1], {"rad": rad + d})

    def update(q, rm, rp, left, right, r, ghost, edge, keep):
        qm = jnp.where(lane == 0, ghost, pltpu.roll(q, 1, 1))
        b = q - qm
        f = jnp.where(lane == NX - 1, edge, pltpu.roll(b, NX - 1, 1))
        slope = jnp.maximum(jnp.minimum(b, f), 0.0) + jnp.minimum(jnp.maximum(b, f), 0.0)
        a = coef[0, r]
        g = a * q + coef[1, r] * slope
        flux_in = jnp.where(lane == 0, a * ghost, pltpu.roll(g, 1, 1))
        cm = jnp.where(sub == 0, left, pltpu.roll(q, 1, 0))
        cp = jnp.where(sub == CC - 1, right, pltpu.roll(q, CC - 1, 0))
        lap = (f - b) + (rm + rp) + (cm + cp) - 4.0 * q
        return q * keep + (flux_in - g) + coef[2, r] * lap

    def sweep(p, v, src, dst, pressures):
        keep = 1.0 - 0.5 * relax[v]
        fresh = []
        for r in range(RC):
            q = src[v, r]
            rm = radr[p, 0, v] if r == 0 else src[v, r - 1]
            rp = radr[p, 1, v] if r == RC - 1 else src[v, r + 1]
            left = axr[p, 0, v, r : r + 1, :]
            right = axr[p, 1, v, r : r + 1, :]
            ghost = pltpu.roll(ghosts[r], lax.rem(NX - v, NX), 1)
            edge = 0.0 if pressures is None else pressures[r] - q
            new = update(q, rm, rp, left, right, r, ghost, edge, keep)
            dst[v, r] = new
            fresh.append(new)
        return fresh

    swirl = None
    for p in range(SWEEPS + 1):
        src = of(p)
        for d in range(1, axes):
            remote(
                ms_src.at[p], ms_own.at[p, ax], s_own.at[p], r_own.at[p], {"ax": lax.rem(ax + d, axes)}
            ).start()
        if p >= 1:

            @pl.when(rad + 1 < rads)
            def _():
                total_copy(p, 1).start()

        @pl.when(rad < rads - 1)
        def _():
            rad_copy(p, True).start()

        @pl.when(rad > 0)
        def _():
            rad_copy(p, False).start()

        ax_copy(p, True).start()
        ax_copy(p, False).start()

        @pl.when(row < rows - 1)
        def _():
            for d in range(axes):
                remote(
                    ms_src.at[p], ms_up.at[p, ax], s_down.at[p], r_up.at[p], {"row": row + 1, "ax": d}
                ).start()

        if p == 1:

            @pl.when(rad + 2 < rads)
            def _():
                pl.semaphore_wait(ready, jnp.minimum(rads - 2 - rad, REACH - 1))

        if p >= 1:
            for d in range(2, REACH):

                @pl.when(rad + d < rads)
                def _():
                    total_copy(p, d).start()

        part = ms_own.at[p, pl.ds(0, axes - 1)]
        remote(part, part, s_own.at[p], r_own.at[p], {"ax": ax}).wait_recv()

        def mean(ref):
            total = ref[p, 0]
            for d in range(1, axes):
                total = total + ref[p, d]
            return total / jnp.broadcast_to(total[:, NV : NV + 1], (8, NX))

        profile = mean(ms_own)
        pressures = None
        if p >= 1:
            for d in range(1, REACH + 1):

                @pl.when(rad >= d)
                def _():
                    total_copy(p, d).wait_recv()

            before = px[p, 0]
            for d in range(2, REACH + 1):
                before = before + px[p, d - 1]
            if p < SWEEPS + 1:
                t_src[p, 1] = before + t_src[p, 0]

                @pl.when(rad + REACH < rads)
                def _():
                    total_copy(p, REACH).start()

            run = swirl
            for step in (1, 2, 4):
                run = run + jnp.where(sub >= step, pltpu.roll(run, step, 0), 0.0)
            scale = 4.0 / (RC * rads)
            pressure = jnp.broadcast_to(profile[:, PV : PV + 1], (8, NX)) + scale * ((run - swirl) + before)
            profile_s[...] = pressure
            rows_of = [profile_s[s : s + 1, :] for s in range(RC)]
            pressures = []
            for r in range(RC):
                st = hot[r]
                acc = jnp.broadcast_to(rows_of[0], (8, NX))
                for s in range(1, RC):
                    acc = jnp.where(st == float(s), rows_of[s], acc)
                pressures.append(acc)
        if p < SWEEPS:
            radius = 1.0 + (rad * RC + sub).astype(jnp.float32) / float(RC * rads)
            third = jnp.broadcast_to(profile[:, SV : SV + 1], (8, NX))
            swirl = third * third / radius
            t_src[p + 1, 0] = jnp.sum(swirl, axis=0, keepdims=True)

        @pl.when(row == 0)
        def _():
            upstream[...] = inlet_t[...]

        @pl.when(row > 0)
        def _():
            remote(ms_up.at[p], ms_up.at[p], s_down.at[p], r_up.at[p], {"ax": ax}).wait_recv()
            upstream[...] = mean(ms_up)

        for r in range(RC):
            st = hot[r]
            acc = jnp.broadcast_to(upstream[0:1, :], (8, NX))
            for s in range(1, RC):
                acc = jnp.where(st == float(s), upstream[s : s + 1, :], acc)
            ghosts[r] = acc

        @pl.when(rad > 0)
        def _():
            rad_copy(p, True).wait_recv()

        @pl.when(rad < rads - 1)
        def _():
            rad_copy(p, False).wait_recv()

        ax_copy(p, True).wait_recv()
        ax_copy(p, False).wait_recv()

        dst = field.at[p] if p + 1 < SWEEPS else out
        picks = (one,) * RC
        if p < SWEEPS:

            def plain(i, picks):
                v = i + jnp.where(i >= PV, 1, 0)
                fresh = sweep(p, v, src, dst, None)
                if p + 1 == SWEEPS:
                    return picks
                pack(dst, p + 1, v)
                return tuple(jnp.where(lane == v, tail(fresh[r]), picks[r]) for r in range(RC))

            picks = lax.fori_loop(0, NV - 1, plain, picks)
        if p == 0:
            for r in range(RC):
                field[0, PV, r] = state[PV, r]
        else:
            lagged = field.at[p] if p < SWEEPS else out
            fresh = sweep(p, PV, src, lagged, pressures)
        if p < SWEEPS:
            lagged = field.at[p]
            pack(lagged, p + 1, PV)
            picks = tuple(jnp.where(lane == PV, tail(lagged[PV, r]), picks[r]) for r in range(RC))
            sums(picks, p + 1)

        if p >= SWEEPS - 1:
            for v in range(NV):
                if (v == PV) == (p == SWEEPS):
                    wide = jnp.broadcast_to(profile[:, v : v + 1], (8, NX))
                    line = jnp.sum(jnp.where(diagonal, wide, 0.0), axis=0, keepdims=True)
                    out_profile[v : v + 1, :] = line[:, :RC]
            if p == SWEEPS:
                line = jnp.sum(jnp.where(diagonal, pressure, 0.0), axis=0, keepdims=True)
                out_pressure[...] = line[:, :RC]

    for p in range(SWEEPS + 1):
        part = ms_own.at[p, pl.ds(0, axes - 1)]
        remote(part, part, s_own.at[p], r_own.at[p], {"ax": ax}).wait_send()

        @pl.when(row < rows - 1)
        def _():
            remote(ms_up.at[p], ms_up.at[p], s_down.at[p], r_up.at[p], {"ax": ax}).wait_send()

        @pl.when(rad < rads - 1)
        def _():
            rad_copy(p, True).wait_send()

        @pl.when(rad > 0)
        def _():
            rad_copy(p, False).wait_send()

        ax_copy(p, True).wait_send()
        ax_copy(p, False).wait_send()
        if p >= 1:
            for d in range(1, REACH + 1):

                @pl.when(rad + d < rads)
                def _():
                    total_copy(p, d).wait_send()


def solution(mesh):
    sizes = (mesh.shape["row"], mesh.shape["rad"], mesh.shape["ax"])
    axes = sizes[2]
    phases = SWEEPS + 1

    def body(state, speed, visc, relax, area, station, flags, inlet):
        vmem = pl.BlockSpec(memory_space=pltpu.VMEM)
        smem = pl.BlockSpec(memory_space=pltpu.SMEM)
        f32 = jnp.float32
        dma = pltpu.SemaphoreType.DMA
        new, profile, pressure = pl.pallas_call(
            functools.partial(kernel, sizes),
            out_shape=(
                jax.ShapeDtypeStruct((NV, RC, CC, NX), f32),
                jax.ShapeDtypeStruct((NV, RC), f32),
                jax.ShapeDtypeStruct((1, RC), f32),
            ),
            in_specs=[vmem, vmem, vmem, smem, vmem, vmem, vmem, vmem],
            out_specs=(vmem, vmem, vmem),
            scratch_shapes=[
                pltpu.VMEM((SWEEPS, NV, RC, CC, NX), f32),
                pltpu.VMEM((phases, 2, NV, RC, NX), f32),
                pltpu.VMEM((phases, 2, NV, RC, NX), f32),
                pltpu.VMEM((phases, 2, NV, CC, NX), f32),
                pltpu.VMEM((phases, RC, NX), f32),
                pltpu.VMEM((phases, axes, RC, NX), f32),
                pltpu.VMEM((phases, axes, RC, NX), f32),
                pltpu.VMEM((phases, 2, 1, NX), f32),
                pltpu.VMEM((phases, REACH, 1, NX), f32),
                pltpu.VMEM((3, RC, CC, NX), f32),
                pltpu.VMEM((RC, RC, CC, NX), f32),
                pltpu.VMEM((RC, CC, NX), f32),
                pltpu.VMEM((RC, NX), f32),
                pltpu.VMEM((RC, NX), f32),
                pltpu.VMEM((RC, CC, NX), f32),
                pltpu.VMEM((RC, NX), f32),
                dma((phases, 2)),
                dma((phases, 2)),
                dma((phases, 2)),
                dma((phases, 2)),
                dma((phases,)),
                dma((phases,)),
                dma((phases,)),
                dma((phases,)),
                dma((phases, REACH)),
                dma((phases, REACH)),
                pltpu.SemaphoreType.REGULAR,
            ],
            compiler_params=pltpu.CompilerParams(
                collective_id=0, has_side_effects=True, vmem_limit_bytes=16 * 1024 * 1024
            ),
        )(
            state.reshape(NV, RC, CC, NX),
            speed.reshape(RC, CC, NX),
            visc.reshape(RC, CC, NX),
            relax,
            area.reshape(RC, CC),
            station.reshape(RC, CC),
            flags.reshape(RC, CC),
            inlet,
        )
        return new[:, None], profile[:, None], pressure

    return jax.shard_map(
        body,
        mesh=mesh,
        in_specs=(
            P(None, "row", "rad", "ax", None),
            P("row", "rad", "ax", None),
            P("row", "rad", "ax", None),
            P(),
            P("row", "rad", "ax"),
            P("row", "rad", "ax"),
            P("row", "rad", "ax"),
            P(None, "rad"),
        ),
        out_specs=(P(None, "row", "rad", "ax", None), P(None, "row", "rad"), P("row", "rad")),
        check_vma=False,
    )
```

```python
import functools

import jax
import jax.numpy as jnp
from jax import lax
from jax.experimental import pallas as pl
from jax.experimental.pallas import tpu as pltpu
from jax.sharding import PartitionSpec as P

MESH = pl.DeviceIdType.MESH
SWEEPS = 4
NV = 7
PV = 4
SV = 3
RC = 8
CC = 8
NX = 128
BASE = (-1, -1, -1, -1, 2, 2, 2, 5, 4, 6, 6, 7, 7, 10, 9, 8)
DIRECT = 6
TX = 8


def kernel(
    sizes,
    state_h,
    speed_h,
    visc_h,
    relax_h,
    area_h,
    station_h,
    flags_h,
    inlet_h,
    out,
    out_profile,
    out_pressure,
    field,
    axs,
    axr,
    radr,
    ms_src,
    ms_own,
    ms_up,
    t_src,
    px,
    coef,
    weight,
    hot,
    upstream,
    inlet_t,
    ghosts,
    profile_s,
    tm_src,
    tm_own,
    tr,
    s_ax,
    r_ax,
    s_rad,
    r_rad,
    s_own,
    r_own,
    s_down,
    r_up,
    s_px,
    r_px,
    s_tm,
    r_tm,
    s_tr,
    r_tr,
    ready,
    state,
    speed,
    visc,
    relax,
    area,
    station,
    flags,
    inlet,
    s_in,
):
    rows, rads, axes = sizes
    row, rad, ax = lax.axis_index("row"), lax.axis_index("rad"), lax.axis_index("ax")
    lane = lax.broadcasted_iota(jnp.int32, (8, NX), 1)
    sub = lax.broadcasted_iota(jnp.int32, (8, NX), 0)
    zero = jnp.zeros((8, NX), jnp.float32)

    def remote(src, dst, ssem, rsem, where):
        return pltpu.make_async_remote_copy(
            src_ref=src, dst_ref=dst, send_sem=ssem, recv_sem=rsem, device_id=where, device_id_type=MESH
        )

    barrier = pltpu.get_barrier_semaphore()

    def greet(where):
        pl.semaphore_signal(barrier, inc=1, device_id=where, device_id_type=MESH)

    for d in range(1, axes):
        greet({"ax": lax.rem(ax + d, axes)})

    heard = [[r for r in range(BASE[x] + 1, x)] for x in range(rads)]
    own_pairs = [(r, x) for x in range(rads) for r in heard[x] if r < x - 1]
    sum_pairs = [(BASE[x], x) for x in range(rads) if BASE[x] >= 0]

    def table(values):
        out = jnp.int32(0)
        for i, value in enumerate(values):
            if value:
                out = out + jnp.where(rad == i, value, 0)
        return out

    def among(which):
        mask = sum(1 << r for r in which)
        return (lax.shift_right_logical(jnp.int32(mask), rad) & 1) == 1

    def distances(pairs):
        return [(d, [r for r, x in pairs if x - r == d]) for d in sorted({x - r for r, x in pairs})]

    @pl.when(rad > 0)
    def _():
        greet({"rad": rad - 1})

    @pl.when(rad < rads - 1)
    def _():
        greet({"rad": rad + 1})

    for d, senders in distances(own_pairs + sum_pairs):

        @pl.when(among(senders))
        def _():
            greet({"rad": rad + d})

    @pl.when(row > 0)
    def _():
        for d in range(axes):
            greet({"row": row - 1, "ax": d})

    first_part, second_part = [
        [pltpu.make_async_copy(src, dst, s_in.at[k, i]) for i, (src, dst) in enumerate(pairs)]
        for k, pairs in enumerate(
            (
                (
                    (area_h, area),
                    (station_h, station),
                    (state_h.at[pl.ds(SV, 2)], state.at[pl.ds(SV, 2)]),
                ),
                (
                    (flags_h, flags),
                    (speed_h, speed),
                    (visc_h, visc),
                    (relax_h, relax),
                    (inlet_h, inlet),
                    (state_h.at[pl.ds(0, SV)], state.at[pl.ds(0, SV)]),
                    (state_h.at[pl.ds(PV + 1, NV - PV - 1)], state.at[pl.ds(PV + 1, NV - PV - 1)]),
                ),
            )
        )
    ]
    for load in first_part + second_part:
        load.start()

    @pl.when(rad == 0)
    def _():
        radr[:, 0] = jnp.zeros_like(radr[:, 0])
        tr[:, 0] = jnp.zeros_like(tr[:, 0])

    @pl.when(rad == rads - 1)
    def _():
        radr[:, 1] = jnp.zeros_like(radr[:, 1])
        tr[:, 1] = jnp.zeros_like(tr[:, 1])

    for d in range(1, DIRECT + 1):

        @pl.when(jnp.logical_not(among([x for x in range(rads) if x - d in heard[x]])))
        def _():
            px[:, d - 1] = jnp.zeros_like(px[:, d - 1])

    @pl.when(among([x for x in range(rads) if BASE[x] < 0]))
    def _():
        px[:, DIRECT] = jnp.zeros_like(px[:, DIRECT])

    diagonal = sub == lane

    def column(ref, r):
        wide = jnp.broadcast_to(ref[r : r + 1, :], (8, 8))
        return jnp.broadcast_to(jnp.sum(jnp.where(diagonal[:, :8], wide, 0.0), axis=1, keepdims=True), (8, NX))

    def greeted():
        fixed = [0] * rads
        for _, x in own_pairs + sum_pairs:
            fixed[x] += 1
        for x in range(rads):
            fixed[x] += (x > 0) + (x < rads - 1)
        pl.semaphore_wait(barrier, (axes - 1) + table(fixed) + jnp.where(row < rows - 1, axes, 0))
        for which, pairs in enumerate((own_pairs, sum_pairs)):
            for d, senders in distances(pairs):

                @pl.when(among([r + d for r in senders]))
                def _():
                    pl.semaphore_signal(ready.at[which], inc=1, device_id={"rad": rad - d}, device_id_type=MESH)

    def await_ready(which):
        counts = [0] * rads
        for r, _ in (own_pairs, sum_pairs)[which]:
            counts[r] += 1

        @pl.when(among([r for r in range(rads) if counts[r]]))
        def _():
            pl.semaphore_wait(ready.at[which], table(counts))

    last = SWEEPS

    group = lax.rem(lane, 64) // TX
    half = lane // 64
    spot = lax.rem(lane, TX)

    def tail_pack(rows_of, both):
        acc = zero
        for r in range(RC):
            for h in range(1 if both else 2):
                moved = pltpu.roll(rows_of(h, r), (TX * (r + 1) + 64 * h) % NX, 1)
                acc = jnp.where((group == r) & (half == h), moved, acc)
        if both:
            acc = jnp.where(half == 0, acc, pltpu.roll(acc, 64, 1))
        return acc

    def tail_copy(p, d):
        n = 2 * RC if p < last else RC
        return remote(
            tm_src.at[p, pl.ds(0, n)],
            tm_own.at[p, ax, pl.ds(0, n)],
            s_tm.at[p],
            r_tm.at[p],
            {"ax": lax.rem(ax + d, axes)},
        )

    def tail_all(p):
        n = 2 * RC if p < last else RC
        part = tm_own.at[p, pl.ds(0, axes - 1), pl.ds(0, n)]
        return remote(part, part, s_tm.at[p], r_tm.at[p], {"ax": ax})

    def tail_rad(p, up):
        side = 0 if up else 1
        where = {"rad": rad + 1 if up else rad - 1}
        return remote(
            tm_src.at[p, pl.ds(RC, RC)], tr.at[p, side], s_tr.at[p, side], r_tr.at[p, side], where
        )

    def total_copy(k, d):
        return remote(t_src.at[k, 0], px.at[k, d - 1], s_px.at[k, d - 1], r_px.at[k, d - 1], {"rad": rad + d})

    def sum_copy(k, d):
        where = {"rad": rad + d}
        return remote(t_src.at[k, 1], px.at[k, DIRECT], s_px.at[k, DIRECT + d - 1], r_px.at[k, DIRECT], where)

    own_steps = distances(own_pairs + [(x - 1, x) for x in range(1, rads)])
    sum_steps = distances(sum_pairs)

    for load in first_part:
        load.wait()
    areas = area[...]
    local_station = (station[...] - rad * RC).astype(jnp.float32)
    tail_station = zero
    tail_area = zero
    for r in range(RC):
        st = column(local_station, r)
        ar = column(areas, r)
        hot[r] = st
        for s in range(RC):
            weight[s, r] = jnp.where(st == float(s), ar, 0.0)
        mine = group == r
        tail_station = jnp.where(mine, st, tail_station)
        tail_area = jnp.where(mine & ((spot == TX - 1) | ((spot == TX - 2) & (half == 0))), ar, tail_area)
    counted = (spot == TX - 2) & (half == 0)

    def tail_send(p, q):
        q = jnp.where(counted, 1.0, q)
        total = zero
        for s in range(RC):
            part = jnp.sum(jnp.where(tail_station == float(s), tail_area, 0.0) * q, axis=0, keepdims=True)
            total = jnp.where(sub == s, part, total)
        tm_src[p, 0:RC] = total
        tm_own[p, ax, 0:RC] = total
        for d in range(1, axes):
            tail_copy(p, d).start()
        if p < last:

            @pl.when(rad > 0)
            def _():
                tail_rad(p, False).start()

            @pl.when(rad < rads - 1)
            def _():
                tail_rad(p, True).start()

        if p == last:

            @pl.when(row < rows - 1)
            def _():
                for d in range(axes):
                    up_copy(p, d).start()

    def up_copy(p, d):
        src = tm_src.at[p, pl.ds(0, RC)] if p == last else ms_src.at[p]
        return remote(src, ms_up.at[p, ax], s_down.at[p], r_up.at[p], {"row": row + 1, "ax": d})

    def fold(total):
        for step in (8, 16, 32):
            total = total + pltpu.roll(total, step, 1)
        return total

    def at(x, i):
        return jnp.broadcast_to(x[:, i : i + 1], (8, NX))

    tail = tail_pack(lambda h, r: state[SV + h, r], False)
    tm_src[0, RC:] = tail
    greeted()
    tail_send(0, tail)

    def sums(picks, p):
        total = zero
        for s in range(RC):
            acc = weight[s, 0] * picks[0]
            for r in range(1, RC):
                acc = acc + weight[s, r] * picks[r]
            total = jnp.where(sub == s, jnp.sum(acc, axis=0, keepdims=True), total)
        ms_src[p] = total
        if p == last - 1:
            ms_own[ax] = total

    def pack(src, p, v):
        for r in range(RC):
            axs[p, 0, v, r : r + 1, :] = src[v, r, 0:1, :]
            axs[p, 1, v, r : r + 1, :] = src[v, r, CC - 1 : CC, :]

    def of(p):
        return state if p == 0 else field.at[p - 1]

    def rad_copy(p, up):
        src = of(p)
        edge = RC - 1 if up else 0
        where = {"rad": rad + 1 if up else rad - 1}
        side = 0 if up else 1
        if p == last:
            return remote(src.at[PV, edge], radr.at[p, side, PV], s_rad.at[p, side], r_rad.at[p, side], where)
        return remote(src.at[:, edge], radr.at[p, side], s_rad.at[p, side], r_rad.at[p, side], where)

    def ax_copy(p, up):
        cell = 1 if up else 0
        where = {"ax": lax.rem(ax + (1 if up else axes - 1), axes)}
        side = 0 if up else 1
        if p == last:
            return remote(axs.at[p, cell, PV], axr.at[p, side, PV], s_ax.at[p, side], r_ax.at[p, side], where)
        return remote(axs.at[p, cell], axr.at[p, side], s_ax.at[p, side], r_ax.at[p, side], where)

    def own_copy(d):
        return remote(ms_src.at[last - 1], ms_own.at[ax], s_own, r_own, {"ax": lax.rem(ax + d, axes)})

    def field_send(p):
        if p < last:

            @pl.when(row < rows - 1)
            def _():
                for d in range(axes):
                    up_copy(p, d).start()

        @pl.when(rad < rads - 1)
        def _():
            rad_copy(p, True).start()

        @pl.when(rad > 0)
        def _():
            rad_copy(p, False).start()

        ax_copy(p, True).start()
        ax_copy(p, False).start()
        if p == last - 1:
            for d in range(1, axes):
                own_copy(d).start()

    def update(q, rm, rp, left, right, coefs, ghost, edge, keep):
        a, ah, nu = coefs
        qm = jnp.where(lane == 0, ghost, pltpu.roll(q, 1, 1))
        b = q - qm
        f = jnp.where(lane == NX - 1, edge, pltpu.roll(b, NX - 1, 1))
        slope = jnp.maximum(jnp.minimum(b, f), 0.0) + jnp.minimum(jnp.maximum(b, f), 0.0)
        g = a * q + ah * slope
        flux_in = jnp.where(lane == 0, a * ghost, pltpu.roll(g, 1, 1))
        cm = jnp.where(sub == 0, left, pltpu.roll(q, 1, 0))
        cp = jnp.where(sub == CC - 1, right, pltpu.roll(q, CC - 1, 0))
        lap = (f - b) + (rm + rp) + (cm + cp) - 4.0 * q
        return q * keep + (flux_in - g) + nu * lap

    def tail_update(p, q, ghost):
        left = tm_own[p, lax.rem(ax + axes - 1, axes), 2 * RC - 1 : 2 * RC]
        right = tm_own[p, lax.rem(ax + 1, axes), RC : RC + 1]
        a, ah, nu, keep = tail_coefs
        b = q - pltpu.roll(q, 1, 1)
        edge = 0.0 if ghost is None else jnp.where(half == 0, 0.0, ghost - q)
        f = jnp.where(spot == TX - 1, edge, pltpu.roll(b, NX - 1, 1))
        slope = jnp.maximum(jnp.minimum(b, f), 0.0) + jnp.minimum(jnp.maximum(b, f), 0.0)
        g = a * q + ah * slope
        rm = jnp.where(group == 0, pltpu.roll(tr[p, 0], 72, 1), pltpu.roll(q, TX, 1))
        rp = jnp.where(group == RC - 1, pltpu.roll(tr[p, 1], 56, 1), pltpu.roll(q, NX - TX, 1))
        cm = jnp.where(sub == 0, left, pltpu.roll(q, 1, 0))
        cp = jnp.where(sub == CC - 1, right, pltpu.roll(q, CC - 1, 0))
        lap = (f - b) + (rm + rp) + (cm + cp) - 4.0 * q
        new = q * keep + (pltpu.roll(g, 1, 1) - g) + nu * lap
        return jnp.where(half == 0, new, q) if ghost is None else new

    def sweep(p, v, src, dst, pressures):
        keep = 1.0 - 0.5 * relax[v]
        fresh = []
        for r in range(RC):
            q = src[v, r]
            rm = radr[p, 0, v] if r == 0 else src[v, r - 1]
            rp = radr[p, 1, v] if r == RC - 1 else src[v, r + 1]
            left = axr[p, 0, v, r : r + 1, :]
            right = axr[p, 1, v, r : r + 1, :]
            ghost = pltpu.roll(ghosts[r], (NX - v) % NX if isinstance(v, int) else lax.rem(NX - v, NX), 1)
            edge = 0.0 if pressures is None else pressures[r] - q
            new = update(q, rm, rp, left, right, (coef[0, r], coef[1, r], coef[2, r]), ghost, edge, keep)
            dst[v, r] = new
            fresh.append(new)
        return fresh

    for load in second_part:
        load.wait()
    one = jnp.where(lane == NV, 1.0, 0.0)

    def first(v, picks):
        pack(state, 0, v)
        return tuple(jnp.where(lane == v, at(state[v, r], NX - 1), picks[r]) for r in range(RC))

    sums(lax.fori_loop(0, NV, first, (one,) * RC), 0)
    field_send(0)

    flag = flags[...].astype(jnp.float32)
    tail_flag = zero
    for r in range(RC):
        fl = 0.5 * column(flag, r)
        tail_flag = jnp.where(group == r, fl, tail_flag)
        a = 0.5 * speed[r]
        coef[0, r] = a
        coef[1, r] = a * fl
        coef[2, r] = 0.5 * visc[r]
        field[0, PV, r] = state[PV, r]
    tail_a = tail_pack(lambda h, r: coef[0, r], True)
    tail_coefs = (
        tail_a,
        tail_a * tail_flag,
        tail_pack(lambda h, r: coef[2, r], True),
        1.0 - 0.5 * jnp.where(half == 0, relax[SV], relax[PV]),
    )
    turned = zero
    inlet_all = inlet[...]
    for v in range(NV):
        turned = jnp.where(lane == v, column(inlet_all, v), turned)
    inlet_t[...] = turned
    radius = 1.0 + (rad * RC + sub).astype(jnp.float32) / float(RC * rads)

    def write_profile(v, wide):
        line = jnp.sum(jnp.where(diagonal, wide, 0.0), axis=0, keepdims=True)
        out_profile[v : v + 1, :] = line[:, :RC]

    def total_of(load):
        total = load(0)
        for d in range(1, axes):
            total = total + load(d)
        return total

    swirl = None
    for p in range(SWEEPS + 1):
        tail_all(p).wait_recv()
        if p < last:

            @pl.when(rad > 0)
            def _():
                tail_rad(p, True).wait_recv()

            @pl.when(rad < rads - 1)
            def _():
                tail_rad(p, False).wait_recv()

        folded = fold(total_of(lambda d: tm_own[p, d, 0:RC]))
        areas_in = at(folded, 62)
        ghost = None
        if p >= 1:
            for d, senders in own_steps:

                @pl.when(among([r + d for r in senders]))
                def _():
                    total_copy(p - 1, d).wait_recv()

            @pl.when(among([x for x in range(rads) if BASE[x] >= 0]))
            def _():
                sum_copy(p - 1, 1).wait_recv()

            before = jnp.sum(px[p - 1], axis=0)
            t_src[p - 1, 1] = before + t_src[p - 1, 0]
            if p == 1:
                await_ready(1)
            for d, senders in sum_steps:

                @pl.when(among(senders))
                def _():
                    sum_copy(p - 1, d).start()

            run = swirl
            for step in (1, 2, 4):
                run = run + jnp.where(sub >= step, pltpu.roll(run, step, 0), 0.0)
            scale = 4.0 / (RC * rads)
            fourth = at(folded, 127) / areas_in
            pressure = fourth + scale * ((run - swirl) + before)
            profile_s[...] = pressure
            rows_of = [profile_s[s : s + 1, :] for s in range(RC)]
            if p < last:
                ghost = jnp.broadcast_to(rows_of[0], (8, NX))
                for s in range(1, RC):
                    ghost = jnp.where(tail_station == float(s), rows_of[s], ghost)
        if p < last:
            third = at(folded, 63) / areas_in
            swirl = third * third / radius
            t_src[p, 0] = jnp.sum(swirl, axis=0, keepdims=True)
            tail = tail_update(p, tail, ghost)
            if p + 1 < last:
                tm_src[p + 1, RC:] = tail
            tail_send(p + 1, tail)

            if p == 0:
                await_ready(0)
            for d, senders in own_steps:

                @pl.when(among(senders))
                def _():
                    total_copy(p, d).start()

        src = of(p)

        @pl.when(row == 0)
        def _():
            upstream[...] = inlet_t[...]

        @pl.when(row > 0)
        def _():
            remote(ms_up.at[p], ms_up.at[p], s_down.at[p], r_up.at[p], {"ax": ax}).wait_recv()
            total = total_of(lambda d: ms_up[p, d])
            if p == last:
                total = fold(total)
                upstream[...] = at(total, 127) / at(total, 62)
            else:
                upstream[...] = total / at(total, NV)

        for r in range(RC):
            st = hot[r]
            acc = jnp.broadcast_to(upstream[0:1, :], (8, NX))
            for s in range(1, RC):
                acc = jnp.where(st == float(s), upstream[s : s + 1, :], acc)
            ghosts[r] = acc

        @pl.when(rad > 0)
        def _():
            rad_copy(p, True).wait_recv()

        @pl.when(rad < rads - 1)
        def _():
            rad_copy(p, False).wait_recv()

        ax_copy(p, True).wait_recv()
        ax_copy(p, False).wait_recv()

        dst = field.at[p] if p + 1 < SWEEPS else out
        picks = (one,) * RC
        if p < SWEEPS:

            def plain(i, picks):
                v = i + (1 if i >= PV else 0)
                fresh = sweep(p, v, src, dst, None)
                if p + 1 == SWEEPS:
                    return picks
                pack(dst, p + 1, v)
                return tuple(jnp.where(lane == v, at(fresh[r], NX - 1), picks[r]) for r in range(RC))

            for i in range(NV - 1):
                picks = plain(i, picks)
        if p > 0:
            pressures = []
            for r in range(RC):
                st = hot[r]
                acc = jnp.broadcast_to(rows_of[0], (8, NX))
                for s in range(1, RC):
                    acc = jnp.where(st == float(s), rows_of[s], acc)
                pressures.append(acc)
            fresh = sweep(p, PV, src, field.at[p] if p < SWEEPS else out, pressures)
        else:
            fresh = [state[PV, r] for r in range(RC)]
        if p < SWEEPS:
            pack(field.at[p], p + 1, PV)
            if p + 1 < SWEEPS:
                sums(tuple(jnp.where(lane == PV, at(fresh[r], NX - 1), picks[r]) for r in range(RC)), p + 1)
            field_send(p + 1)

    remote(ms_own.at[pl.ds(0, axes - 1)], ms_own.at[pl.ds(0, axes - 1)], s_own, r_own, {"ax": ax}).wait_recv()
    total = total_of(lambda d: ms_own[d])
    profile = total / at(total, NV)
    for v in range(NV):
        write_profile(v, fourth if v == PV else at(profile, v))
    out_pressure[...] = jnp.sum(jnp.where(diagonal, pressure, 0.0), axis=0, keepdims=True)[:, :RC]

    remote(ms_own.at[pl.ds(0, axes - 1)], ms_own.at[pl.ds(0, axes - 1)], s_own, r_own, {"ax": ax}).wait_send()
    for p in range(SWEEPS + 1):
        tail_all(p).wait_send()

        @pl.when(row < rows - 1)
        def _():
            remote(ms_up.at[p], ms_up.at[p], s_down.at[p], r_up.at[p], {"ax": ax}).wait_send()

        @pl.when(rad < rads - 1)
        def _():
            rad_copy(p, True).wait_send()
            if p < last:
                tail_rad(p, True).wait_send()

        @pl.when(rad > 0)
        def _():
            rad_copy(p, False).wait_send()
            if p < last:
                tail_rad(p, False).wait_send()

        ax_copy(p, True).wait_send()
        ax_copy(p, False).wait_send()
        if p < last:
            for d, senders in own_steps:

                @pl.when(among(senders))
                def _():
                    total_copy(p, d).wait_send()

            for d, senders in sum_steps:

                @pl.when(among(senders))
                def _():
                    sum_copy(p, d).wait_send()


def solution(mesh):
    sizes = (mesh.shape["row"], mesh.shape["rad"], mesh.shape["ax"])
    axes = sizes[2]
    phases = SWEEPS + 1

    def body(state, speed, visc, relax, area, station, flags, inlet):
        vmem = pl.BlockSpec(memory_space=pltpu.VMEM)
        hbm = pl.BlockSpec(memory_space=pltpu.HBM)
        f32 = jnp.float32
        dma = pltpu.SemaphoreType.DMA
        new, profile, pressure = pl.pallas_call(
            functools.partial(kernel, sizes),
            out_shape=(
                jax.ShapeDtypeStruct((NV, RC, CC, NX), f32),
                jax.ShapeDtypeStruct((NV, RC), f32),
                jax.ShapeDtypeStruct((1, RC), f32),
            ),
            in_specs=[hbm] * 8,
            out_specs=(vmem, vmem, vmem),
            scratch_shapes=[
                pltpu.VMEM((SWEEPS, NV, RC, CC, NX), f32),
                pltpu.VMEM((phases, 2, NV, RC, NX), f32),
                pltpu.VMEM((phases, 2, NV, RC, NX), f32),
                pltpu.VMEM((phases, 2, NV, CC, NX), f32),
                pltpu.VMEM((phases, RC, NX), f32),
                pltpu.VMEM((axes, RC, NX), f32),
                pltpu.VMEM((phases, axes, RC, NX), f32),
                pltpu.VMEM((SWEEPS, 2, 1, NX), f32),
                pltpu.VMEM((SWEEPS, DIRECT + 1, 1, NX), f32),
                pltpu.VMEM((3, RC, CC, NX), f32),
                pltpu.VMEM((RC, RC, CC, NX), f32),
                pltpu.VMEM((RC, CC, NX), f32),
                pltpu.VMEM((RC, NX), f32),
                pltpu.VMEM((RC, NX), f32),
                pltpu.VMEM((RC, CC, NX), f32),
                pltpu.VMEM((RC, NX), f32),
                pltpu.VMEM((phases, 2 * RC, NX), f32),
                pltpu.VMEM((phases, axes, 2 * RC, NX), f32),
                pltpu.VMEM((SWEEPS, 2, CC, NX), f32),
                dma((phases, 2)),
                dma((phases, 2)),
                dma((phases, 2)),
                dma((phases, 2)),
                dma,
                dma,
                dma((phases,)),
                dma((phases,)),
                dma((SWEEPS, 2 * DIRECT + 1)),
                dma((SWEEPS, DIRECT + 1)),
                dma((phases,)),
                dma((phases,)),
                dma((SWEEPS, 2)),
                dma((SWEEPS, 2)),
                pltpu.SemaphoreType.REGULAR((2,)),
                pltpu.VMEM((NV, RC, CC, NX), f32),
                pltpu.VMEM((RC, CC, NX), f32),
                pltpu.VMEM((RC, CC, NX), f32),
                pltpu.SMEM((NV,), f32),
                pltpu.VMEM((RC, CC), f32),
                pltpu.VMEM((RC, CC), jnp.int32),
                pltpu.VMEM((RC, CC), jnp.int32),
                pltpu.VMEM((NV, RC), f32),
                dma((2, 8)),
            ],
            compiler_params=pltpu.CompilerParams(
                collective_id=0, has_side_effects=True, vmem_limit_bytes=16 * 1024 * 1024
            ),
        )(
            *[
                pltpu.with_memory_space_constraint(x, pltpu.HBM)
                for x in (
                    state.reshape(NV, RC, CC, NX),
                    speed.reshape(RC, CC, NX),
                    visc.reshape(RC, CC, NX),
                    relax,
                    area.reshape(RC, CC),
                    station.reshape(RC, CC),
                    flags.reshape(RC, CC),
                    inlet,
                )
            ]
        )
        return new[:, None], profile[:, None], pressure

    return jax.shard_map(
        body,
        mesh=mesh,
        in_specs=(
            P(None, "row", "rad", "ax", None),
            P("row", "rad", "ax", None),
            P("row", "rad", "ax", None),
            P(),
            P("row", "rad", "ax"),
            P("row", "rad", "ax"),
            P("row", "rad", "ax"),
            P(None, "rad"),
        ),
        out_specs=(P(None, "row", "rad", "ax", None), P(None, "row", "rad"), P("row", "rad")),
        check_vma=False,
    )
```

```python
import functools

import jax
import jax.numpy as jnp
from jax import lax
from jax.experimental import pallas as pl
from jax.experimental.pallas import tpu as pltpu
from jax.sharding import PartitionSpec as P

MESH = pl.DeviceIdType.MESH
SWEEPS = 4
NV = 7
PV = 4
SV = 3
RC = 8
CC = 8
NX = 128
BASE = (-1, -1, -1, -1, 1, 3, 2, 4, 4, 6, 6, 6, 7, 8, 10, 9)
DIRECT = 6
TX = 8


def kernel(
    sizes,
    state_h,
    speed_h,
    visc_h,
    relax_h,
    area_h,
    station_h,
    flags_h,
    inlet_h,
    out,
    out_profile,
    out_pressure,
    field,
    axs,
    axr,
    radr,
    ms_src,
    ms_own,
    ms_up,
    t_src,
    px,
    coef,
    weight,
    hot,
    upstream,
    inlet_t,
    ghosts,
    profile_s,
    tm_src,
    tm_own,
    tr,
    nb_src,
    nb_in,
    s_ax,
    r_ax,
    s_rad,
    r_rad,
    s_own,
    r_own,
    s_down,
    r_up,
    s_px,
    r_px,
    s_tm,
    r_tm,
    s_tr,
    r_tr,
    s_nb,
    r_nb,
    ready,
    state,
    speed,
    visc,
    relax,
    area,
    station,
    flags,
    inlet,
    s_in,
):
    rows, rads, axes = sizes
    row, rad, ax = lax.axis_index("row"), lax.axis_index("rad"), lax.axis_index("ax")
    lane = lax.broadcasted_iota(jnp.int32, (8, NX), 1)
    sub = lax.broadcasted_iota(jnp.int32, (8, NX), 0)
    zero = jnp.zeros((8, NX), jnp.float32)

    def remote(src, dst, ssem, rsem, where):
        return pltpu.make_async_remote_copy(
            src_ref=src, dst_ref=dst, send_sem=ssem, recv_sem=rsem, device_id=where, device_id_type=MESH
        )

    barrier = pltpu.get_barrier_semaphore()

    def greet(where):
        pl.semaphore_signal(barrier, inc=1, device_id=where, device_id_type=MESH)

    for d in range(1, axes):
        greet({"ax": lax.rem(ax + d, axes)})

    heard = [[r for r in range(BASE[x] + 1, x)] for x in range(rads)]
    own_pairs = [(r, x) for x in range(rads) for r in heard[x] if r < x - 1]
    sum_pairs = [(BASE[x], x) for x in range(rads) if BASE[x] >= 0]

    def table(values):
        out = jnp.int32(0)
        for i, value in enumerate(values):
            if value:
                out = out + jnp.where(rad == i, value, 0)
        return out

    def among(which):
        mask = sum(1 << r for r in which)
        return (lax.shift_right_logical(jnp.int32(mask), rad) & 1) == 1

    def distances(pairs):
        return [(d, [r for r, x in pairs if x - r == d]) for d in sorted({x - r for r, x in pairs})]

    around = [lax.rem(ax + axes - 1, axes), ax, lax.rem(ax + 1, axes)]

    @pl.when(rad > 0)
    def _():
        for where in around:
            greet({"rad": rad - 1, "ax": where})

    @pl.when(rad < rads - 1)
    def _():
        for where in around:
            greet({"rad": rad + 1, "ax": where})

    for d, senders in distances(own_pairs + sum_pairs):

        @pl.when(among(senders))
        def _():
            greet({"rad": rad + d})

    @pl.when(row > 0)
    def _():
        for d in range(axes):
            greet({"row": row - 1, "ax": d})

    first_part, second_part = [
        [pltpu.make_async_copy(src, dst, s_in.at[k, i]) for i, (src, dst) in enumerate(pairs)]
        for k, pairs in enumerate(
            (
                (
                    (state_h.at[pl.ds(SV, 2)], state.at[pl.ds(SV, 2)]),
                    (speed_h, speed),
                    (visc_h, visc),
                    (area_h, area),
                    (station_h, station),
                    (flags_h, flags),
                ),
                (
                    (relax_h, relax),
                    (inlet_h, inlet),
                    (state_h.at[pl.ds(0, SV)], state.at[pl.ds(0, SV)]),
                    (state_h.at[pl.ds(PV + 1, NV - PV - 1)], state.at[pl.ds(PV + 1, NV - PV - 1)]),
                ),
            )
        )
    ]
    for load in first_part + second_part:
        load.start()

    @pl.when(rad == 0)
    def _():
        radr[:, 0] = jnp.zeros_like(radr[:, 0])
        tr[:, 0] = jnp.zeros_like(tr[:, 0])
        nb_in[0] = jnp.zeros_like(nb_in[0])

    @pl.when(rad == rads - 1)
    def _():
        radr[:, 1] = jnp.zeros_like(radr[:, 1])
        tr[:, 1] = jnp.zeros_like(tr[:, 1])
        nb_in[2] = jnp.zeros_like(nb_in[2])

    for d in range(1, DIRECT + 1):

        @pl.when(jnp.logical_not(among([x for x in range(rads) if x - d in heard[x]])))
        def _():
            px[:, d - 1] = jnp.zeros_like(px[:, d - 1])

    @pl.when(among([x for x in range(rads) if BASE[x] < 0]))
    def _():
        px[:, DIRECT] = jnp.zeros_like(px[:, DIRECT])

    diagonal = sub == lane

    def column(ref, r):
        wide = jnp.broadcast_to(ref[r : r + 1, :], (8, 8))
        return jnp.broadcast_to(jnp.sum(jnp.where(diagonal[:, :8], wide, 0.0), axis=1, keepdims=True), (8, NX))

    def greeted():
        fixed = [0] * rads
        for _, x in own_pairs + sum_pairs:
            fixed[x] += 1
        for x in range(rads):
            fixed[x] += 3 * (x > 0) + 3 * (x < rads - 1)
        pl.semaphore_wait(barrier, (axes - 1) + table(fixed) + jnp.where(row < rows - 1, axes, 0))
        for which, pairs in enumerate((own_pairs, sum_pairs)):
            for d, senders in distances(pairs):

                @pl.when(among([r + d for r in senders]))
                def _():
                    pl.semaphore_signal(ready.at[which], inc=1, device_id={"rad": rad - d}, device_id_type=MESH)

    def await_ready(which):
        counts = [0] * rads
        for r, _ in (own_pairs, sum_pairs)[which]:
            counts[r] += 1

        @pl.when(among([r for r in range(rads) if counts[r]]))
        def _():
            pl.semaphore_wait(ready.at[which], table(counts))

    last = SWEEPS

    group = lane // TX
    spot = lax.rem(lane, TX)
    middle = (group >= 4) & (group < 12)

    def doubled(x):
        return jnp.where(middle, x, pltpu.roll(x, 64, 1))

    def tail_pack(row_of):
        acc = zero
        for r in range(RC):
            acc = jnp.where(group == r + 4, pltpu.roll(row_of(r), (TX * (r + 5)) % NX, 1), acc)
        return doubled(acc)

    def wide(p):
        return 2 * RC if p in (2, 3) else RC

    def tail_copy(p, d):
        n = wide(p)
        return remote(
            tm_src.at[p, pl.ds(0, n)],
            tm_own.at[p, ax, pl.ds(0, n)],
            s_tm.at[p],
            r_tm.at[p],
            {"ax": lax.rem(ax + d, axes)},
        )

    def tail_all(p):
        part = tm_own.at[p, pl.ds(0, axes - 1), pl.ds(0, wide(p))]
        return remote(part, part, s_tm.at[p], r_tm.at[p], {"ax": ax})

    def tail_rad(p, up):
        side = 0 if up else 1
        where = {"rad": rad + 1 if up else rad - 1}
        return remote(
            tm_src.at[p, pl.ds(RC, RC)], tr.at[p, side], s_tr.at[p, side], r_tr.at[p, side], where
        )

    def near_copy(i, j):
        n = 3 * i + j
        where = {"rad": rad + 1 - i, "ax": around[2 - j]}
        return remote(nb_src, nb_in.at[i, j], s_nb.at[n], r_nb.at[n], where)

    def near_each(action, sent):
        for j in (1, 0, 2):
            for i in (1, 0, 2):
                if i == 1 and j == 1:
                    continue
                if i == 1:
                    action(near_copy(i, j))
                elif (i == 0) == sent:

                    @pl.when(rad < rads - 1)
                    def _():
                        action(near_copy(i, j))

                else:

                    @pl.when(rad > 0)
                    def _():
                        action(near_copy(i, j))

    def total_copy(k, d):
        return remote(t_src.at[k, 0], px.at[k, d - 1], s_px.at[k, d - 1], r_px.at[k, d - 1], {"rad": rad + d})

    def sum_copy(k, d):
        where = {"rad": rad + d}
        return remote(t_src.at[k, 1], px.at[k, DIRECT], s_px.at[k, DIRECT + d - 1], r_px.at[k, DIRECT], where)

    own_steps = distances(own_pairs + [(x - 1, x) for x in range(1, rads)])
    sum_steps = distances(sum_pairs)

    for load in first_part:
        load.wait()
    areas = area[...]
    local_station = (station[...] - rad * RC).astype(jnp.float32)
    tail_station = zero
    tail_area = zero
    for r in range(RC):
        st = column(local_station, r)
        ar = column(areas, r)
        hot[r] = st
        for s in range(RC):
            weight[s, r] = jnp.where(st == float(s), ar, 0.0)
        mine = group == r + 4
        tail_station = jnp.where(mine, st, tail_station)
        tail_area = jnp.where(mine & (spot >= TX - 3), ar, tail_area)

    def tail_sums(last_one, middle_one, first_one):
        q = jnp.where(spot == TX - 1, last_one, zero)
        q = jnp.where(spot == TX - 2, middle_one, q)
        q = jnp.where(spot == TX - 3, first_one, q)
        total = zero
        for s in range(RC):
            part = jnp.sum(jnp.where(tail_station == float(s), tail_area, 0.0) * q, axis=0, keepdims=True)
            total = jnp.where(sub == s, part, total)
        return total

    def back(x, by):
        return pltpu.roll(x, NX - by, 1)

    def tail_send(p, total):
        tm_src[p, 0:RC] = total
        tm_own[p, ax, 0:RC] = total
        for d in range(1, axes):
            tail_copy(p, d).start()
        if wide(p) > RC:

            @pl.when(rad > 0)
            def _():
                tail_rad(p, False).start()

            @pl.when(rad < rads - 1)
            def _():
                tail_rad(p, True).start()

        if p == last:

            @pl.when(row < rows - 1)
            def _():
                for d in range(axes):
                    up_copy(p, d).start()

    def up_copy(p, d):
        src = tm_src.at[p, pl.ds(0, RC)] if p == last else ms_src.at[p]
        return remote(src, ms_up.at[p, ax], s_down.at[p], r_up.at[p], {"row": row + 1, "ax": d})

    def fold(total):
        for step in (8, 16, 32):
            total = total + pltpu.roll(total, step, 1)
        return total

    def at(x, i):
        return jnp.broadcast_to(x[:, i : i + 1], (8, NX))

    flag = flags[...].astype(jnp.float32)
    tail_flag = zero
    for r in range(RC):
        fl = 0.5 * column(flag, r)
        tail_flag = jnp.where(group == r + 4, fl, tail_flag)
        a = 0.5 * speed[r]
        coef[0, r] = a
        coef[1, r] = a * fl
        coef[2, r] = 0.5 * visc[r]
    tails = [
        tail_pack(lambda r: state[SV, r]),
        tail_pack(lambda r: state[PV, r]),
        tail_pack(lambda r: coef[0, r]),
        tail_pack(lambda r: coef[2, r]),
        doubled(tail_flag),
    ]
    for i, x in enumerate(tails):
        nb_src[i] = x
    greeted()
    tail_send(0, tail_sums(tails[0], 1.0, back(tails[1], 2)))
    near_each(lambda copy: copy.start(), True)
    tail = tails[1]

    def sums(picks, p):
        total = zero
        for s in range(RC):
            acc = weight[s, 0] * picks[0]
            for r in range(1, RC):
                acc = acc + weight[s, r] * picks[r]
            total = jnp.where(sub == s, jnp.sum(acc, axis=0, keepdims=True), total)
        ms_src[p] = total
        if p == last - 1:
            ms_own[ax] = total

    def pack(src, p, v):
        for r in range(RC):
            axs[p, 0, v, r : r + 1, :] = src[v, r, 0:1, :]
            axs[p, 1, v, r : r + 1, :] = src[v, r, CC - 1 : CC, :]

    def of(p):
        return state if p == 0 else field.at[p - 1]

    def rad_copy(p, up):
        src = of(p)
        edge = RC - 1 if up else 0
        where = {"rad": rad + 1 if up else rad - 1}
        side = 0 if up else 1
        if p == last:
            return remote(src.at[PV, edge], radr.at[p, side, PV], s_rad.at[p, side], r_rad.at[p, side], where)
        return remote(src.at[:, edge], radr.at[p, side], s_rad.at[p, side], r_rad.at[p, side], where)

    def ax_copy(p, up):
        cell = 1 if up else 0
        where = {"ax": lax.rem(ax + (1 if up else axes - 1), axes)}
        side = 0 if up else 1
        if p == last:
            return remote(axs.at[p, cell, PV], axr.at[p, side, PV], s_ax.at[p, side], r_ax.at[p, side], where)
        return remote(axs.at[p, cell], axr.at[p, side], s_ax.at[p, side], r_ax.at[p, side], where)

    def own_copy(d):
        return remote(ms_src.at[last - 1], ms_own.at[ax], s_own, r_own, {"ax": lax.rem(ax + d, axes)})

    def field_send(p):
        if p < last:

            @pl.when(row < rows - 1)
            def _():
                for d in range(axes):
                    up_copy(p, d).start()

        @pl.when(rad < rads - 1)
        def _():
            rad_copy(p, True).start()

        @pl.when(rad > 0)
        def _():
            rad_copy(p, False).start()

        ax_copy(p, True).start()
        ax_copy(p, False).start()
        if p == last - 1:
            for d in range(1, axes):
                own_copy(d).start()

    def update(q, rm, rp, left, right, coefs, ghost, edge, keep):
        a, ah, nu = coefs
        qm = jnp.where(lane == 0, ghost, pltpu.roll(q, 1, 1))
        b = q - qm
        f = jnp.where(lane == NX - 1, edge, pltpu.roll(b, NX - 1, 1))
        slope = jnp.maximum(jnp.minimum(b, f), 0.0) + jnp.minimum(jnp.maximum(b, f), 0.0)
        g = a * q + ah * slope
        flux_in = jnp.where(lane == 0, a * ghost, pltpu.roll(g, 1, 1))
        cm = jnp.where(sub == 0, left, pltpu.roll(q, 1, 0))
        cp = jnp.where(sub == CC - 1, right, pltpu.roll(q, CC - 1, 0))
        lap = (f - b) + (rm + rp) + (cm + cp) - 4.0 * q
        return q * keep + (flux_in - g) + nu * lap

    def tail_step(q, lower, upper, cm, cp, coefs, keep, edge):
        a, ah, nu = coefs
        b = q - pltpu.roll(q, 1, 1)
        f = jnp.where(spot == TX - 1, edge, back(b, 1))
        slope = jnp.maximum(jnp.minimum(b, f), 0.0) + jnp.minimum(jnp.maximum(b, f), 0.0)
        g = a * q + ah * slope
        lap = (f - b) + (lower + upper) + (cm + cp) - 4.0 * q
        return q * keep + (pltpu.roll(g, 1, 1) - g) + nu * lap

    def tail_update(p, q, ghost):
        if p == 1:
            lo, hi, left, right = [nb_in[i, j, 1] for i, j in ((0, 1), (2, 1), (1, 0), (1, 2))]
        else:
            lo, hi = tr[p, 0], tr[p, 1]
            left, right = [tm_own[p, around[j], RC : 2 * RC] for j in (0, 2)]
        full = jnp.where(group < 4, lo, jnp.where(group < 12, q, hi))
        cm = jnp.where(sub == 0, left[CC - 1 : CC], pltpu.roll(q, 1, 0))
        cp = jnp.where(sub == CC - 1, right[0:1], pltpu.roll(q, CC - 1, 0))
        coefs = (tails[2], tails[2] * tails[4], tails[3])
        keep = 1.0 - 0.5 * relax[PV]
        new = tail_step(q, pltpu.roll(full, TX, 1), back(full, TX), cm, cp, coefs, keep, ghost - q)
        return doubled(new)

    def deep(i):
        def comb(j):
            own = tails[i] if j == 1 else nb_in[1, j, i]
            return jnp.where(group < 4, nb_in[0, j, i], jnp.where(group < 12, own, nb_in[2, j, i]))

        return comb(1), jnp.where(sub < 4, comb(2), comb(0))

    def deep_sections():
        pair = deep(0)
        a, nu, fl = deep(2), deep(3), deep(4)
        keep = 1.0 - 0.5 * relax[SV]
        found = []
        for _ in range(SWEEPS - 1):
            new = []
            for h in range(2):
                q, other = pair[h], pair[1 - h]
                cm = jnp.where(sub == 0, other[CC - 1 : CC], pltpu.roll(q, 1, 0))
                cp = jnp.where(sub == CC - 1, other[0:1], pltpu.roll(q, CC - 1, 0))
                coefs = (a[h], a[h] * fl[h], nu[h])
                new.append(tail_step(q, pltpu.roll(q, TX, 1), back(q, TX), cm, cp, coefs, keep, 0.0))
            pair = new
            found.append(pair[0])
        return found

    def sweep(p, v, src, dst, pressures):
        keep = 1.0 - 0.5 * relax[v]
        fresh = []
        for r in range(RC):
            q = src[v, r]
            rm = radr[p, 0, v] if r == 0 else src[v, r - 1]
            rp = radr[p, 1, v] if r == RC - 1 else src[v, r + 1]
            left = axr[p, 0, v, r : r + 1, :]
            right = axr[p, 1, v, r : r + 1, :]
            ghost = pltpu.roll(ghosts[r], (NX - v) % NX if isinstance(v, int) else lax.rem(NX - v, NX), 1)
            edge = 0.0 if pressures is None else pressures[r] - q
            new = update(q, rm, rp, left, right, (coef[0, r], coef[1, r], coef[2, r]), ghost, edge, keep)
            dst[v, r] = new
            fresh.append(new)
        return fresh

    for load in second_part:
        load.wait()
    one = jnp.where(lane == NV, 1.0, 0.0)

    def first(v, picks):
        pack(state, 0, v)
        return tuple(jnp.where(lane == v, at(state[v, r], NX - 1), picks[r]) for r in range(RC))

    sums(lax.fori_loop(0, NV, first, (one,) * RC), 0)
    field_send(0)

    for r in range(RC):
        field[0, PV, r] = state[PV, r]
    turned = zero
    inlet_all = inlet[...]
    for v in range(NV):
        turned = jnp.where(lane == v, column(inlet_all, v), turned)
    inlet_t[...] = turned
    radius = 1.0 + (rad * RC + sub).astype(jnp.float32) / float(RC * rads)

    def write_profile(v, wide):
        line = jnp.sum(jnp.where(diagonal, wide, 0.0), axis=0, keepdims=True)
        out_profile[v] = line[:, :RC]

    def total_of(load):
        total = load(0)
        for d in range(1, axes):
            total = total + load(d)
        return total

    def send_totals(batch):
        for k in batch:
            for d, senders in own_steps:

                @pl.when(among(senders))
                def _():
                    total_copy(k, d).start()

    def totals_in(batch):
        for k in batch:
            for d, senders in own_steps:

                @pl.when(among([r + d for r in senders]))
                def _():
                    total_copy(k, d).wait_recv()

            @pl.when(among([x for x in range(rads) if BASE[x] >= 0]))
            def _():
                sum_copy(k, 1).wait_recv()

        before = []
        for k in batch:
            before.append(jnp.sum(px[k], axis=0))
            t_src[k, 1] = before[-1] + t_src[k, 0]
        if batch[0] == 0:
            await_ready(1)
        for d, senders in sum_steps:

            @pl.when(among(senders))
            def _():
                for k in batch:
                    sum_copy(k, d).start()

        return before

    scale = 4.0 / (RC * rads)
    swirls, befores = [], []

    def add_swirl(third):
        swirls.append(third * third / radius)
        t_src[len(swirls) - 1, 0] = jnp.sum(swirls[-1], axis=0, keepdims=True)

    for p in range(SWEEPS + 1):
        tail_all(p).wait_recv()
        folded = fold(total_of(lambda d: tm_own[p, d, 0:RC]))
        if p == 0:
            areas_in = at(folded, 94)
            fourth = at(folded, 93) / areas_in
            add_swirl(at(folded, 95) / areas_in)
            await_ready(0)
            send_totals((0,))
            near_each(lambda copy: copy.wait_recv(), False)
            one_on, two_on, three_on = deep_sections()
            tail_send(1, tail_sums(one_on, back(two_on, 1), back(three_on, 2)))
        else:
            if p == 1:
                for i in (95, 94, 93):
                    add_swirl(at(folded, i) / areas_in)
                send_totals((1, 2, 3))
            else:
                fourth = at(folded, 95) / areas_in
            if wide(p) > RC:

                @pl.when(rad > 0)
                def _():
                    tail_rad(p, True).wait_recv()

                @pl.when(rad < rads - 1)
                def _():
                    tail_rad(p, False).wait_recv()

            run = swirls[p - 1]
            for step in (1, 2, 4):
                run = run + jnp.where(sub >= step, pltpu.roll(run, step, 0), 0.0)
            pressure = fourth + scale * ((run - swirls[p - 1]) + befores[p - 1])
            profile_s[...] = pressure
            rows_of = [profile_s[s : s + 1, :] for s in range(RC)]
            if p < last:
                ghost = jnp.broadcast_to(rows_of[0], (8, NX))
                for s in range(1, RC):
                    ghost = jnp.where(tail_station == float(s), rows_of[s], ghost)
                tail = tail_update(p, tail, ghost)
                if wide(p + 1) > RC:
                    tm_src[p + 1, RC:] = tail
                tail_send(p + 1, tail_sums(tail, 1.0, zero))

        src = of(p)

        @pl.when(row == 0)
        def _():
            upstream[...] = inlet_t[...]

        @pl.when(row > 0)
        def _():
            remote(ms_up.at[p], ms_up.at[p], s_down.at[p], r_up.at[p], {"ax": ax}).wait_recv()
            total = total_of(lambda d: ms_up[p, d])
            if p == last:
                total = fold(total)
                upstream[...] = at(total, 95) / at(total, 94)
            else:
                upstream[...] = total / at(total, NV)

        for r in range(RC):
            st = hot[r]
            acc = jnp.broadcast_to(upstream[0:1, :], (8, NX))
            for s in range(1, RC):
                acc = jnp.where(st == float(s), upstream[s : s + 1, :], acc)
            ghosts[r] = acc

        @pl.when(rad > 0)
        def _():
            rad_copy(p, True).wait_recv()

        @pl.when(rad < rads - 1)
        def _():
            rad_copy(p, False).wait_recv()

        ax_copy(p, True).wait_recv()
        ax_copy(p, False).wait_recv()

        dst = field.at[p] if p + 1 < SWEEPS else out
        picks = (one,) * RC
        if p < SWEEPS:

            def plain(i, picks):
                v = i + (1 if i >= PV else 0)
                fresh = sweep(p, v, src, dst, None)
                if p + 1 == SWEEPS:
                    return picks
                pack(dst, p + 1, v)
                return tuple(jnp.where(lane == v, at(fresh[r], NX - 1), picks[r]) for r in range(RC))

            for i in range(NV - 1):
                picks = plain(i, picks)
        if p > 0:
            pressures = []
            for r in range(RC):
                st = hot[r]
                acc = jnp.broadcast_to(rows_of[0], (8, NX))
                for s in range(1, RC):
                    acc = jnp.where(st == float(s), rows_of[s], acc)
                pressures.append(acc)
            fresh = sweep(p, PV, src, field.at[p] if p < SWEEPS else out, pressures)
        else:
            fresh = [state[PV, r] for r in range(RC)]
        if p < SWEEPS:
            pack(field.at[p], p + 1, PV)
            if p + 1 < SWEEPS:
                sums(tuple(jnp.where(lane == PV, at(fresh[r], NX - 1), picks[r]) for r in range(RC)), p + 1)
            field_send(p + 1)
        if p == 0:
            befores += totals_in((0,))
        if p == 1:
            befores += totals_in((1, 2, 3))

    remote(ms_own.at[pl.ds(0, axes - 1)], ms_own.at[pl.ds(0, axes - 1)], s_own, r_own, {"ax": ax}).wait_recv()
    total = total_of(lambda d: ms_own[d])
    profile = total / at(total, NV)
    for v in range(NV):
        write_profile(v, fourth if v == PV else at(profile, v))
    out_pressure[...] = jnp.sum(jnp.where(diagonal, pressure, 0.0), axis=0, keepdims=True)[:, :RC]

    near_each(lambda copy: copy.wait_send(), True)
    remote(ms_own.at[pl.ds(0, axes - 1)], ms_own.at[pl.ds(0, axes - 1)], s_own, r_own, {"ax": ax}).wait_send()
    for p in range(SWEEPS + 1):
        tail_all(p).wait_send()

        @pl.when(row < rows - 1)
        def _():
            remote(ms_up.at[p], ms_up.at[p], s_down.at[p], r_up.at[p], {"ax": ax}).wait_send()

        @pl.when(rad < rads - 1)
        def _():
            rad_copy(p, True).wait_send()
            if wide(p) > RC:
                tail_rad(p, True).wait_send()

        @pl.when(rad > 0)
        def _():
            rad_copy(p, False).wait_send()
            if wide(p) > RC:
                tail_rad(p, False).wait_send()

        ax_copy(p, True).wait_send()
        ax_copy(p, False).wait_send()
        if p < last:
            for d, senders in own_steps:

                @pl.when(among(senders))
                def _():
                    total_copy(p, d).wait_send()

            for d, senders in sum_steps:

                @pl.when(among(senders))
                def _():
                    sum_copy(p, d).wait_send()


def store(new, profile, pressure, out, out_profile, out_pressure, sems):
    copies = [
        pltpu.make_async_copy(src, dst, sems.at[i])
        for i, (src, dst) in enumerate(((new, out), (profile, out_profile), (pressure, out_pressure)))
    ]
    for copy in copies:
        copy.start()
    for copy in copies:
        copy.wait()


def solution(mesh):
    sizes = (mesh.shape["row"], mesh.shape["rad"], mesh.shape["ax"])
    axes = sizes[2]
    phases = SWEEPS + 1

    def body(state, speed, visc, relax, area, station, flags, inlet):
        vmem = pl.BlockSpec(memory_space=pltpu.VMEM)
        hbm = pl.BlockSpec(memory_space=pltpu.HBM)
        f32 = jnp.float32
        dma = pltpu.SemaphoreType.DMA
        new, profile, pressure = pl.pallas_call(
            functools.partial(kernel, sizes),
            out_shape=(
                jax.ShapeDtypeStruct((NV, RC, CC, NX), f32),
                jax.ShapeDtypeStruct((NV, 1, RC), f32),
                jax.ShapeDtypeStruct((1, RC), f32),
            ),
            in_specs=[hbm] * 8,
            out_specs=(vmem, vmem, vmem),
            scratch_shapes=[
                pltpu.VMEM((SWEEPS, NV, RC, CC, NX), f32),
                pltpu.VMEM((phases, 2, NV, RC, NX), f32),
                pltpu.VMEM((phases, 2, NV, RC, NX), f32),
                pltpu.VMEM((phases, 2, NV, CC, NX), f32),
                pltpu.VMEM((phases, RC, NX), f32),
                pltpu.VMEM((axes, RC, NX), f32),
                pltpu.VMEM((phases, axes, RC, NX), f32),
                pltpu.VMEM((SWEEPS, 2, 1, NX), f32),
                pltpu.VMEM((SWEEPS, DIRECT + 1, 1, NX), f32),
                pltpu.VMEM((3, RC, CC, NX), f32),
                pltpu.VMEM((RC, RC, CC, NX), f32),
                pltpu.VMEM((RC, CC, NX), f32),
                pltpu.VMEM((RC, NX), f32),
                pltpu.VMEM((RC, NX), f32),
                pltpu.VMEM((RC, CC, NX), f32),
                pltpu.VMEM((RC, NX), f32),
                pltpu.VMEM((phases, 2 * RC, NX), f32),
                pltpu.VMEM((phases, axes, 2 * RC, NX), f32),
                pltpu.VMEM((SWEEPS, 2, CC, NX), f32),
                pltpu.VMEM((5, CC, NX), f32),
                pltpu.VMEM((3, 3, 5, CC, NX), f32),
                dma((phases, 2)),
                dma((phases, 2)),
                dma((phases, 2)),
                dma((phases, 2)),
                dma,
                dma,
                dma((phases,)),
                dma((phases,)),
                dma((SWEEPS, 2 * DIRECT + 1)),
                dma((SWEEPS, DIRECT + 1)),
                dma((phases,)),
                dma((phases,)),
                dma((SWEEPS, 2)),
                dma((SWEEPS, 2)),
                dma((9,)),
                dma((9,)),
                pltpu.SemaphoreType.REGULAR((2,)),
                pltpu.VMEM((NV, RC, CC, NX), f32),
                pltpu.VMEM((RC, CC, NX), f32),
                pltpu.VMEM((RC, CC, NX), f32),
                pltpu.SMEM((NV,), f32),
                pltpu.VMEM((RC, CC), f32),
                pltpu.VMEM((RC, CC), jnp.int32),
                pltpu.VMEM((RC, CC), jnp.int32),
                pltpu.VMEM((NV, RC), f32),
                dma((2, 8)),
            ],
            compiler_params=pltpu.CompilerParams(
                collective_id=0, has_side_effects=True, vmem_limit_bytes=16 * 1024 * 1024
            ),
        )(
            *[
                pltpu.with_memory_space_constraint(x, pltpu.HBM)
                for x in (
                    state.reshape(NV, RC, CC, NX),
                    speed.reshape(RC, CC, NX),
                    visc.reshape(RC, CC, NX),
                    relax,
                    area.reshape(RC, CC),
                    station.reshape(RC, CC),
                    flags.reshape(RC, CC),
                    inlet,
                )
            ]
        )
        new, profile, pressure = pl.pallas_call(
            store,
            out_shape=(
                jax.ShapeDtypeStruct((NV, RC, CC, NX), f32),
                jax.ShapeDtypeStruct((NV, 1, RC), f32),
                jax.ShapeDtypeStruct((1, RC), f32),
            ),
            in_specs=[vmem] * 3,
            out_specs=(hbm,) * 3,
            scratch_shapes=[dma((3,))],
            compiler_params=pltpu.CompilerParams(vmem_limit_bytes=4 * 1024 * 1024),
        )(new, profile, pressure)
        return new[:, None], profile, pressure

    return jax.shard_map(
        body,
        mesh=mesh,
        in_specs=(
            P(None, "row", "rad", "ax", None),
            P("row", "rad", "ax", None),
            P("row", "rad", "ax", None),
            P(),
            P("row", "rad", "ax"),
            P("row", "rad", "ax"),
            P("row", "rad", "ax"),
            P(None, "rad"),
        ),
        out_specs=(P(None, "row", "rad", "ax", None), P(None, "row", "rad"), P("row", "rad")),
        check_vma=False,
    )
```

```python
import functools

import jax
import jax.numpy as jnp
from jax import lax
from jax.experimental import pallas as pl
from jax.experimental.pallas import tpu as pltpu
from jax.sharding import PartitionSpec as P

MESH = pl.DeviceIdType.MESH
SWEEPS = 4
NV = 7
PV = 4
SV = 3
RC = 8
CC = 8
NX = 128
BASE = (-1, -1, -1, -1, 1, 3, 2, 4, 4, 6, 6, 6, 7, 8, 10, 9)
DIRECT = 6
TX = 8


def kernel(
    sizes,
    state_h,
    speed_h,
    visc_h,
    relax_h,
    area_h,
    station_h,
    flags_h,
    inlet_h,
    out,
    out_profile,
    out_pressure,
    field,
    axs,
    axr,
    radr,
    ms_src,
    ms_own,
    ms_up,
    t_src,
    px,
    coef,
    weight,
    hot,
    upstream,
    inlet_t,
    ghosts,
    profile_s,
    tm_src,
    tm_own,
    tr,
    nb_src,
    nb_in,
    s_ax,
    r_ax,
    s_rad,
    r_rad,
    s_own,
    r_own,
    s_down,
    r_up,
    s_px,
    r_px,
    s_tm,
    r_tm,
    s_tr,
    r_tr,
    s_nb,
    r_nb,
    ready,
    state,
    speed,
    visc,
    relax,
    area,
    station,
    flags,
    inlet,
    s_in,
):
    rows, rads, axes = sizes
    row, rad, ax = lax.axis_index("row"), lax.axis_index("rad"), lax.axis_index("ax")
    lane = lax.broadcasted_iota(jnp.int32, (8, NX), 1)
    sub = lax.broadcasted_iota(jnp.int32, (8, NX), 0)
    zero = jnp.zeros((8, NX), jnp.float32)

    def remote(src, dst, ssem, rsem, where):
        return pltpu.make_async_remote_copy(
            src_ref=src, dst_ref=dst, send_sem=ssem, recv_sem=rsem, device_id=where, device_id_type=MESH
        )

    barrier = pltpu.get_barrier_semaphore()

    def greet(where):
        pl.semaphore_signal(barrier, inc=1, device_id=where, device_id_type=MESH)

    for d in range(1, axes):
        greet({"ax": lax.rem(ax + d, axes)})

    heard = [[r for r in range(BASE[x] + 1, x)] for x in range(rads)]
    own_pairs = [(r, x) for x in range(rads) for r in heard[x] if r < x - 1]
    sum_pairs = [(BASE[x], x) for x in range(rads) if BASE[x] >= 0]

    def table(values):
        out = jnp.int32(0)
        for i, value in enumerate(values):
            if value:
                out = out + jnp.where(rad == i, value, 0)
        return out

    def among(which):
        mask = sum(1 << r for r in which)
        return (lax.shift_right_logical(jnp.int32(mask), rad) & 1) == 1

    def distances(pairs):
        return [(d, [r for r, x in pairs if x - r == d]) for d in sorted({x - r for r, x in pairs}, reverse=True)]

    around = [lax.rem(ax + axes - 1, axes), ax, lax.rem(ax + 1, axes)]

    @pl.when(rad > 0)
    def _():
        for where in around:
            greet({"rad": rad - 1, "ax": where})

    @pl.when(rad < rads - 1)
    def _():
        for where in around:
            greet({"rad": rad + 1, "ax": where})

    for d, senders in distances(own_pairs + sum_pairs):

        @pl.when(among(senders))
        def _():
            greet({"rad": rad + d})

    @pl.when(row > 0)
    def _():
        for d in range(axes):
            greet({"row": row - 1, "ax": d})

    first_part, second_part = [
        [pltpu.make_async_copy(src, dst, s_in.at[k, i]) for i, (src, dst) in enumerate(pairs)]
        for k, pairs in enumerate(
            (
                (
                    (state_h.at[pl.ds(SV, 2)], state.at[pl.ds(SV, 2)]),
                    (speed_h, speed),
                    (visc_h, visc),
                    (area_h, area),
                    (station_h, station),
                    (flags_h, flags),
                ),
                (
                    (relax_h, relax),
                    (inlet_h, inlet),
                    (state_h.at[pl.ds(0, SV)], state.at[pl.ds(0, SV)]),
                    (state_h.at[pl.ds(PV + 1, NV - PV - 1)], state.at[pl.ds(PV + 1, NV - PV - 1)]),
                ),
            )
        )
    ]
    for load in first_part + second_part:
        load.start()

    @pl.when(rad == 0)
    def _():
        radr[:, 0] = jnp.zeros_like(radr[:, 0])
        tr[:, 0] = jnp.zeros_like(tr[:, 0])
        nb_in[0] = jnp.zeros_like(nb_in[0])

    @pl.when(rad == rads - 1)
    def _():
        radr[:, 1] = jnp.zeros_like(radr[:, 1])
        tr[:, 1] = jnp.zeros_like(tr[:, 1])
        nb_in[2] = jnp.zeros_like(nb_in[2])

    for d in range(1, DIRECT + 1):

        @pl.when(jnp.logical_not(among([x for x in range(rads) if x - d in heard[x]])))
        def _():
            px[:, d - 1] = jnp.zeros_like(px[:, d - 1])

    @pl.when(among([x for x in range(rads) if BASE[x] < 0]))
    def _():
        px[:, DIRECT] = jnp.zeros_like(px[:, DIRECT])

    diagonal = sub == lane

    def column(ref, r):
        wide = jnp.broadcast_to(ref[r : r + 1, :], (8, 8))
        return jnp.broadcast_to(jnp.sum(jnp.where(diagonal[:, :8], wide, 0.0), axis=1, keepdims=True), (8, NX))

    partners = sorted(range(1, axes), key=lambda d: (-min(d, axes - d), d))

    def greeted():
        fixed = [0] * rads
        for _, x in own_pairs + sum_pairs:
            fixed[x] += 1
        for x in range(rads):
            fixed[x] += 3 * (x > 0) + 3 * (x < rads - 1)
        pl.semaphore_wait(barrier, (axes - 1) + table(fixed) + jnp.where(row < rows - 1, axes, 0))
        for which, pairs in enumerate((own_pairs, sum_pairs)):
            for d, senders in distances(pairs):

                @pl.when(among([r + d for r in senders]))
                def _():
                    pl.semaphore_signal(ready.at[which], inc=1, device_id={"rad": rad - d}, device_id_type=MESH)

    def await_ready(which):
        counts = [0] * rads
        for r, _ in (own_pairs, sum_pairs)[which]:
            counts[r] += 1

        @pl.when(among([r for r in range(rads) if counts[r]]))
        def _():
            pl.semaphore_wait(ready.at[which], table(counts))

    last = SWEEPS

    group = lane // TX
    spot = lax.rem(lane, TX)
    middle = (group >= 4) & (group < 12)

    def doubled(x):
        return jnp.where(middle, x, pltpu.roll(x, 64, 1))

    def tail_pack(row_of):
        acc = zero
        for r in range(RC):
            acc = jnp.where(group == r + 4, pltpu.roll(row_of(r), (TX * (r + 5)) % NX, 1), acc)
        return doubled(acc)

    def wide(p):
        return 2 * RC if p in (2, 3) else RC

    def tail_copy(p, d):
        n = wide(p)
        return remote(
            tm_src.at[p, pl.ds(0, n)],
            tm_own.at[p, ax, pl.ds(0, n)],
            s_tm.at[p],
            r_tm.at[p],
            {"ax": lax.rem(ax + d, axes)},
        )

    def tail_all(p):
        part = tm_own.at[p, pl.ds(0, axes - 1), pl.ds(0, wide(p))]
        return remote(part, part, s_tm.at[p], r_tm.at[p], {"ax": ax})

    def tail_rad(p, up):
        side = 0 if up else 1
        where = {"rad": rad + 1 if up else rad - 1}
        return remote(
            tm_src.at[p, pl.ds(RC, RC)], tr.at[p, side], s_tr.at[p, side], r_tr.at[p, side], where
        )

    def near_copy(i, j):
        n = 3 * i + j
        where = {"rad": rad + 1 - i, "ax": around[2 - j]}
        return remote(nb_src, nb_in.at[i, j], s_nb.at[n], r_nb.at[n], where)

    def near_each(action, sent):
        for j in (0, 2, 1):
            for i in (0, 2, 1):
                if i == 1 and j == 1:
                    continue
                if i == 1:
                    action(near_copy(i, j))
                elif (i == 0) == sent:

                    @pl.when(rad < rads - 1)
                    def _():
                        action(near_copy(i, j))

                else:

                    @pl.when(rad > 0)
                    def _():
                        action(near_copy(i, j))

    def total_copy(k, d):
        return remote(t_src.at[k, 0], px.at[k, d - 1], s_px.at[k, d - 1], r_px.at[k, d - 1], {"rad": rad + d})

    def sum_copy(k, d):
        where = {"rad": rad + d}
        return remote(t_src.at[k, 1], px.at[k, DIRECT], s_px.at[k, DIRECT + d - 1], r_px.at[k, DIRECT], where)

    own_steps = distances(own_pairs + [(x - 1, x) for x in range(1, rads)])
    sum_steps = distances(sum_pairs)

    for load in first_part:
        load.wait()
    areas = area[...]
    local_station = (station[...] - rad * RC).astype(jnp.float32)
    tail_station = zero
    tail_area = zero
    for r in range(RC):
        st = column(local_station, r)
        ar = column(areas, r)
        hot[r] = st
        for s in range(RC):
            weight[s, r] = jnp.where(st == float(s), ar, 0.0)
        mine = group == r + 4
        tail_station = jnp.where(mine, st, tail_station)
        tail_area = jnp.where(mine & (spot >= TX - 3), ar, tail_area)

    def tail_sums(last_one, middle_one, first_one):
        q = jnp.where(spot == TX - 1, last_one, zero)
        q = jnp.where(spot == TX - 2, middle_one, q)
        q = jnp.where(spot == TX - 3, first_one, q)
        total = zero
        for s in range(RC):
            part = jnp.sum(jnp.where(tail_station == float(s), tail_area, 0.0) * q, axis=0, keepdims=True)
            total = jnp.where(sub == s, part, total)
        return total

    def back(x, by):
        return pltpu.roll(x, NX - by, 1)

    def tail_send(p, total):
        tm_src[p, 0:RC] = total
        tm_own[p, ax, 0:RC] = total
        for d in partners:
            tail_copy(p, d).start()
        if wide(p) > RC:

            @pl.when(rad > 0)
            def _():
                tail_rad(p, False).start()

            @pl.when(rad < rads - 1)
            def _():
                tail_rad(p, True).start()

        if p == last:

            @pl.when(row < rows - 1)
            def _():
                for d in partners + [0]:
                    up_copy(p, d).start()

    def up_copy(p, d):
        src = tm_src.at[p, pl.ds(0, RC)] if p == last else ms_src.at[p]
        return remote(src, ms_up.at[p, ax], s_down.at[p], r_up.at[p], {"row": row + 1, "ax": lax.rem(ax + d, axes)})

    def fold(total):
        for step in (8, 16, 32):
            total = total + pltpu.roll(total, step, 1)
        return total

    def at(x, i):
        return jnp.broadcast_to(x[:, i : i + 1], (8, NX))

    flag = flags[...].astype(jnp.float32)
    tail_flag = zero
    for r in range(RC):
        fl = 0.5 * column(flag, r)
        tail_flag = jnp.where(group == r + 4, fl, tail_flag)
        a = 0.5 * speed[r]
        coef[0, r] = a
        coef[1, r] = a * fl
        coef[2, r] = 0.5 * visc[r]
    tails = [
        tail_pack(lambda r: state[SV, r]),
        tail_pack(lambda r: state[PV, r]),
        tail_pack(lambda r: coef[0, r]),
        tail_pack(lambda r: coef[2, r]),
        doubled(tail_flag),
    ]
    for i, x in enumerate(tails):
        nb_src[i] = x
    greeted()
    tail_send(0, tail_sums(tails[0], 1.0, back(tails[1], 2)))
    near_each(lambda copy: copy.start(), True)
    tail = tails[1]

    def sums(picks, p):
        total = zero
        for s in range(RC):
            acc = weight[s, 0] * picks[0]
            for r in range(1, RC):
                acc = acc + weight[s, r] * picks[r]
            total = jnp.where(sub == s, jnp.sum(acc, axis=0, keepdims=True), total)
        ms_src[p] = total
        if p == last - 1:
            ms_own[ax] = total

    def pack(src, p, v):
        for r in range(RC):
            axs[p, 0, v, r : r + 1, :] = src[v, r, 0:1, :]
            axs[p, 1, v, r : r + 1, :] = src[v, r, CC - 1 : CC, :]

    def of(p):
        return state if p == 0 else field.at[p - 1]

    def rad_copy(p, up):
        src = of(p)
        edge = RC - 1 if up else 0
        where = {"rad": rad + 1 if up else rad - 1}
        side = 0 if up else 1
        if p == last:
            return remote(src.at[PV, edge], radr.at[p, side, PV], s_rad.at[p, side], r_rad.at[p, side], where)
        return remote(src.at[:, edge], radr.at[p, side], s_rad.at[p, side], r_rad.at[p, side], where)

    def ax_copy(p, up):
        cell = 1 if up else 0
        where = {"ax": lax.rem(ax + (1 if up else axes - 1), axes)}
        side = 0 if up else 1
        if p == last:
            return remote(axs.at[p, cell, PV], axr.at[p, side, PV], s_ax.at[p, side], r_ax.at[p, side], where)
        return remote(axs.at[p, cell], axr.at[p, side], s_ax.at[p, side], r_ax.at[p, side], where)

    def own_copy(d):
        return remote(ms_src.at[last - 1], ms_own.at[ax], s_own, r_own, {"ax": lax.rem(ax + d, axes)})

    def field_send(p):
        if p < last:

            @pl.when(row < rows - 1)
            def _():
                for d in partners + [0]:
                    up_copy(p, d).start()

        @pl.when(rad < rads - 1)
        def _():
            rad_copy(p, True).start()

        @pl.when(rad > 0)
        def _():
            rad_copy(p, False).start()

        ax_copy(p, True).start()
        ax_copy(p, False).start()
        if p == last - 1:
            for d in partners:
                own_copy(d).start()

    def update(q, rm, rp, left, right, coefs, ghost, edge, keep):
        a, ah, nu = coefs
        qm = jnp.where(lane == 0, ghost, pltpu.roll(q, 1, 1))
        b = q - qm
        f = jnp.where(lane == NX - 1, edge, pltpu.roll(b, NX - 1, 1))
        slope = jnp.maximum(jnp.minimum(b, f), 0.0) + jnp.minimum(jnp.maximum(b, f), 0.0)
        g = a * q + ah * slope
        flux_in = jnp.where(lane == 0, a * ghost, pltpu.roll(g, 1, 1))
        cm = jnp.where(sub == 0, left, pltpu.roll(q, 1, 0))
        cp = jnp.where(sub == CC - 1, right, pltpu.roll(q, CC - 1, 0))
        lap = (f - b) + (rm + rp) + (cm + cp) - 4.0 * q
        return q * keep + (flux_in - g) + nu * lap

    def tail_step(q, lower, upper, cm, cp, coefs, keep, edge):
        a, ah, nu = coefs
        b = q - pltpu.roll(q, 1, 1)
        f = jnp.where(spot == TX - 1, edge, back(b, 1))
        slope = jnp.maximum(jnp.minimum(b, f), 0.0) + jnp.minimum(jnp.maximum(b, f), 0.0)
        g = a * q + ah * slope
        lap = (f - b) + (lower + upper) + (cm + cp) - 4.0 * q
        return q * keep + (pltpu.roll(g, 1, 1) - g) + nu * lap

    def tail_update(p, q, ghost):
        if p == 1:
            lo, hi, left, right = [nb_in[i, j, 1] for i, j in ((0, 1), (2, 1), (1, 0), (1, 2))]
        else:
            lo, hi = tr[p, 0], tr[p, 1]
            left, right = [tm_own[p, around[j], RC : 2 * RC] for j in (0, 2)]
        full = jnp.where(group < 4, lo, jnp.where(group < 12, q, hi))
        cm = jnp.where(sub == 0, left[CC - 1 : CC], pltpu.roll(q, 1, 0))
        cp = jnp.where(sub == CC - 1, right[0:1], pltpu.roll(q, CC - 1, 0))
        coefs = (tails[2], tails[2] * tails[4], tails[3])
        keep = 1.0 - 0.5 * relax[PV]
        new = tail_step(q, pltpu.roll(full, TX, 1), back(full, TX), cm, cp, coefs, keep, ghost - q)
        return doubled(new)

    def deep(i):
        def comb(j):
            own = tails[i] if j == 1 else nb_in[1, j, i]
            return jnp.where(group < 4, nb_in[0, j, i], jnp.where(group < 12, own, nb_in[2, j, i]))

        return comb(1), jnp.where(sub < 4, comb(2), comb(0))

    def deep_sections():
        pair = deep(0)
        a, nu, fl = deep(2), deep(3), deep(4)
        keep = 1.0 - 0.5 * relax[SV]
        found = []
        for _ in range(SWEEPS - 1):
            new = []
            for h in range(2):
                q, other = pair[h], pair[1 - h]
                cm = jnp.where(sub == 0, other[CC - 1 : CC], pltpu.roll(q, 1, 0))
                cp = jnp.where(sub == CC - 1, other[0:1], pltpu.roll(q, CC - 1, 0))
                coefs = (a[h], a[h] * fl[h], nu[h])
                new.append(tail_step(q, pltpu.roll(q, TX, 1), back(q, TX), cm, cp, coefs, keep, 0.0))
            pair = new
            found.append(pair[0])
        return found

    def sweep(p, v, src, dst, pressures):
        keep = 1.0 - 0.5 * relax[v]
        fresh = []
        for r in range(RC):
            q = src[v, r]
            rm = radr[p, 0, v] if r == 0 else src[v, r - 1]
            rp = radr[p, 1, v] if r == RC - 1 else src[v, r + 1]
            left = axr[p, 0, v, r : r + 1, :]
            right = axr[p, 1, v, r : r + 1, :]
            ghost = pltpu.roll(ghosts[r], (NX - v) % NX if isinstance(v, int) else lax.rem(NX - v, NX), 1)
            edge = 0.0 if pressures is None else pressures[r] - q
            new = update(q, rm, rp, left, right, (coef[0, r], coef[1, r], coef[2, r]), ghost, edge, keep)
            dst[v, r] = new
            fresh.append(new)
        return fresh

    for load in second_part:
        load.wait()
    one = jnp.where(lane == NV, 1.0, 0.0)

    def first(v, picks):
        pack(state, 0, v)
        return tuple(jnp.where(lane == v, at(state[v, r], NX - 1), picks[r]) for r in range(RC))

    sums(lax.fori_loop(0, NV, first, (one,) * RC), 0)
    field_send(0)

    for r in range(RC):
        field[0, PV, r] = state[PV, r]
    turned = zero
    inlet_all = inlet[...]
    for v in range(NV):
        turned = jnp.where(lane == v, column(inlet_all, v), turned)
    inlet_t[...] = turned
    radius = 1.0 + (rad * RC + sub).astype(jnp.float32) / float(RC * rads)

    def write_profile(v, wide):
        line = jnp.sum(jnp.where(diagonal, wide, 0.0), axis=0, keepdims=True)
        out_profile[v] = line[:, :RC]

    def total_of(load):
        total = load(0)
        for d in range(1, axes):
            total = total + load(d)
        return total

    def send_totals(batch):
        for k in batch:
            for d, senders in own_steps:

                @pl.when(among(senders))
                def _():
                    total_copy(k, d).start()

    def totals_in(batch):
        for k in batch:
            for d, senders in own_steps:

                @pl.when(among([r + d for r in senders]))
                def _():
                    total_copy(k, d).wait_recv()

            @pl.when(among([x for x in range(rads) if BASE[x] >= 0]))
            def _():
                sum_copy(k, 1).wait_recv()

        before = []
        for k in batch:
            before.append(jnp.sum(px[k], axis=0))
            t_src[k, 1] = before[-1] + t_src[k, 0]
        if batch[0] == 0:
            await_ready(1)
        for d, senders in sum_steps:

            @pl.when(among(senders))
            def _():
                for k in batch:
                    sum_copy(k, d).start()

        return before

    scale = 4.0 / (RC * rads)
    swirls, befores = [], []

    def add_swirl(third):
        swirls.append(third * third / radius)
        t_src[len(swirls) - 1, 0] = jnp.sum(swirls[-1], axis=0, keepdims=True)

    def sent(p):
        tail_all(p).wait_send()

        @pl.when(row < rows - 1)
        def _():
            remote(ms_up.at[p], ms_up.at[p], s_down.at[p], r_up.at[p], {"ax": ax}).wait_send()

        @pl.when(rad < rads - 1)
        def _():
            rad_copy(p, True).wait_send()
            if wide(p) > RC:
                tail_rad(p, True).wait_send()

        @pl.when(rad > 0)
        def _():
            rad_copy(p, False).wait_send()
            if wide(p) > RC:
                tail_rad(p, False).wait_send()

        ax_copy(p, True).wait_send()
        ax_copy(p, False).wait_send()

    def totals_sent(k):
        for d, senders in own_steps:

            @pl.when(among(senders))
            def _():
                total_copy(k, d).wait_send()

        for d, senders in sum_steps:

            @pl.when(among(senders))
            def _():
                sum_copy(k, d).wait_send()

    own_part = ms_own.at[pl.ds(0, axes - 1)]
    own_all = remote(own_part, own_part, s_own, r_own, {"ax": ax})

    for p in range(SWEEPS + 1):
        if p == last:
            own_all.wait_recv()
            total = total_of(lambda d: ms_own[d])
            profile = total / at(total, NV)
            for v in range(NV):
                if v != PV:
                    write_profile(v, at(profile, v))
            own_all.wait_send()
            sent(p - 1)

        tail_all(p).wait_recv()
        folded = fold(total_of(lambda d: tm_own[p, d, 0:RC]))
        if p == 0:
            areas_in = at(folded, 94)
            fourth = at(folded, 93) / areas_in
            add_swirl(at(folded, 95) / areas_in)
            await_ready(0)
            send_totals((0,))
            near_each(lambda copy: copy.wait_recv(), False)
            one_on, two_on, three_on = deep_sections()
            tail_send(1, tail_sums(one_on, back(two_on, 1), back(three_on, 2)))
        else:
            if p == 1:
                for i in (95, 94, 93):
                    add_swirl(at(folded, i) / areas_in)
                send_totals((1, 2, 3))
            else:
                fourth = at(folded, 95) / areas_in
            if wide(p) > RC:

                @pl.when(rad > 0)
                def _():
                    tail_rad(p, True).wait_recv()

                @pl.when(rad < rads - 1)
                def _():
                    tail_rad(p, False).wait_recv()

            run = swirls[p - 1]
            for step in (1, 2, 4):
                run = run + jnp.where(sub >= step, pltpu.roll(run, step, 0), 0.0)
            pressure = fourth + scale * ((run - swirls[p - 1]) + befores[p - 1])
            profile_s[...] = pressure
            rows_of = [profile_s[s : s + 1, :] for s in range(RC)]
            if p < last:
                ghost = jnp.broadcast_to(rows_of[0], (8, NX))
                for s in range(1, RC):
                    ghost = jnp.where(tail_station == float(s), rows_of[s], ghost)
                tail = tail_update(p, tail, ghost)
                if wide(p + 1) > RC:
                    tm_src[p + 1, RC:] = tail
                tail_send(p + 1, tail_sums(tail, 1.0, zero))

        src = of(p)

        @pl.when(row == 0)
        def _():
            upstream[...] = inlet_t[...]

        @pl.when(row > 0)
        def _():
            remote(ms_up.at[p], ms_up.at[p], s_down.at[p], r_up.at[p], {"ax": ax}).wait_recv()
            total = total_of(lambda d: ms_up[p, d])
            if p == last:
                total = fold(total)
                upstream[...] = at(total, 95) / at(total, 94)
            else:
                upstream[...] = total / at(total, NV)

        for r in range(RC):
            st = hot[r]
            acc = jnp.broadcast_to(upstream[0:1, :], (8, NX))
            for s in range(1, RC):
                acc = jnp.where(st == float(s), upstream[s : s + 1, :], acc)
            ghosts[r] = acc

        @pl.when(rad > 0)
        def _():
            rad_copy(p, True).wait_recv()

        @pl.when(rad < rads - 1)
        def _():
            rad_copy(p, False).wait_recv()

        ax_copy(p, True).wait_recv()
        ax_copy(p, False).wait_recv()

        dst = field.at[p] if p + 1 < SWEEPS else out
        picks = (one,) * RC
        if p < SWEEPS:

            def plain(i, picks):
                v = i + (1 if i >= PV else 0)
                fresh = sweep(p, v, src, dst, None)
                if p + 1 == SWEEPS:
                    return picks
                pack(dst, p + 1, v)
                return tuple(jnp.where(lane == v, at(fresh[r], NX - 1), picks[r]) for r in range(RC))

            for i in range(NV - 1):
                picks = plain(i, picks)
        if p > 0:
            pressures = []
            for r in range(RC):
                st = hot[r]
                acc = jnp.broadcast_to(rows_of[0], (8, NX))
                for s in range(1, RC):
                    acc = jnp.where(st == float(s), rows_of[s], acc)
                pressures.append(acc)
            fresh = sweep(p, PV, src, field.at[p] if p < SWEEPS else out, pressures)
        else:
            fresh = [state[PV, r] for r in range(RC)]
        if p < SWEEPS:
            pack(field.at[p], p + 1, PV)
            if p + 1 < SWEEPS:
                sums(tuple(jnp.where(lane == PV, at(fresh[r], NX - 1), picks[r]) for r in range(RC)), p + 1)
            field_send(p + 1)
        if p == 0:
            befores += totals_in((0,))
        if p == 1:
            befores += totals_in((1, 2, 3))
            near_each(lambda copy: copy.wait_send(), True)
        if 1 <= p < last:
            sent(p - 1)
        if p == 2:
            totals_sent(0)
            totals_sent(1)
        if p == 3:
            totals_sent(2)
            totals_sent(3)

    write_profile(PV, fourth)
    out_pressure[...] = jnp.sum(jnp.where(diagonal, pressure, 0.0), axis=0, keepdims=True)[:, :RC]
    sent(last)


def store(new, profile, pressure, out, out_profile, out_pressure, sems):
    copies = [
        pltpu.make_async_copy(src, dst, sems.at[i])
        for i, (src, dst) in enumerate(((new, out), (profile, out_profile), (pressure, out_pressure)))
    ]
    for copy in copies:
        copy.start()
    for copy in copies:
        copy.wait()


def solution(mesh):
    sizes = (mesh.shape["row"], mesh.shape["rad"], mesh.shape["ax"])
    axes = sizes[2]
    phases = SWEEPS + 1

    def body(state, speed, visc, relax, area, station, flags, inlet):
        vmem = pl.BlockSpec(memory_space=pltpu.VMEM)
        hbm = pl.BlockSpec(memory_space=pltpu.HBM)
        f32 = jnp.float32
        dma = pltpu.SemaphoreType.DMA
        new, profile, pressure = pl.pallas_call(
            functools.partial(kernel, sizes),
            out_shape=(
                jax.ShapeDtypeStruct((NV, RC, CC, NX), f32),
                jax.ShapeDtypeStruct((NV, 1, RC), f32),
                jax.ShapeDtypeStruct((1, RC), f32),
            ),
            in_specs=[hbm] * 8,
            out_specs=(vmem, vmem, vmem),
            scratch_shapes=[
                pltpu.VMEM((SWEEPS, NV, RC, CC, NX), f32),
                pltpu.VMEM((phases, 2, NV, RC, NX), f32),
                pltpu.VMEM((phases, 2, NV, RC, NX), f32),
                pltpu.VMEM((phases, 2, NV, CC, NX), f32),
                pltpu.VMEM((phases, RC, NX), f32),
                pltpu.VMEM((axes, RC, NX), f32),
                pltpu.VMEM((phases, axes, RC, NX), f32),
                pltpu.VMEM((SWEEPS, 2, 1, NX), f32),
                pltpu.VMEM((SWEEPS, DIRECT + 1, 1, NX), f32),
                pltpu.VMEM((3, RC, CC, NX), f32),
                pltpu.VMEM((RC, RC, CC, NX), f32),
                pltpu.VMEM((RC, CC, NX), f32),
                pltpu.VMEM((RC, NX), f32),
                pltpu.VMEM((RC, NX), f32),
                pltpu.VMEM((RC, CC, NX), f32),
                pltpu.VMEM((RC, NX), f32),
                pltpu.VMEM((phases, 2 * RC, NX), f32),
                pltpu.VMEM((phases, axes, 2 * RC, NX), f32),
                pltpu.VMEM((SWEEPS, 2, CC, NX), f32),
                pltpu.VMEM((5, CC, NX), f32),
                pltpu.VMEM((3, 3, 5, CC, NX), f32),
                dma((phases, 2)),
                dma((phases, 2)),
                dma((phases, 2)),
                dma((phases, 2)),
                dma,
                dma,
                dma((phases,)),
                dma((phases,)),
                dma((SWEEPS, 2 * DIRECT + 1)),
                dma((SWEEPS, DIRECT + 1)),
                dma((phases,)),
                dma((phases,)),
                dma((SWEEPS, 2)),
                dma((SWEEPS, 2)),
                dma((9,)),
                dma((9,)),
                pltpu.SemaphoreType.REGULAR((2,)),
                pltpu.VMEM((NV, RC, CC, NX), f32),
                pltpu.VMEM((RC, CC, NX), f32),
                pltpu.VMEM((RC, CC, NX), f32),
                pltpu.SMEM((NV,), f32),
                pltpu.VMEM((RC, CC), f32),
                pltpu.VMEM((RC, CC), jnp.int32),
                pltpu.VMEM((RC, CC), jnp.int32),
                pltpu.VMEM((NV, RC), f32),
                dma((2, 8)),
            ],
            compiler_params=pltpu.CompilerParams(
                collective_id=0, has_side_effects=True, vmem_limit_bytes=16 * 1024 * 1024
            ),
        )(
            *[
                pltpu.with_memory_space_constraint(x, pltpu.HBM)
                for x in (
                    state.reshape(NV, RC, CC, NX),
                    speed.reshape(RC, CC, NX),
                    visc.reshape(RC, CC, NX),
                    relax,
                    area.reshape(RC, CC),
                    station.reshape(RC, CC),
                    flags.reshape(RC, CC),
                    inlet,
                )
            ]
        )
        new, profile, pressure = pl.pallas_call(
            store,
            out_shape=(
                jax.ShapeDtypeStruct((NV, RC, CC, NX), f32),
                jax.ShapeDtypeStruct((NV, 1, RC), f32),
                jax.ShapeDtypeStruct((1, RC), f32),
            ),
            in_specs=[vmem] * 3,
            out_specs=(hbm,) * 3,
            scratch_shapes=[dma((3,))],
            compiler_params=pltpu.CompilerParams(vmem_limit_bytes=4 * 1024 * 1024),
        )(new, profile, pressure)
        return new[:, None], profile, pressure

    return jax.shard_map(
        body,
        mesh=mesh,
        in_specs=(
            P(None, "row", "rad", "ax", None),
            P("row", "rad", "ax", None),
            P("row", "rad", "ax", None),
            P(),
            P("row", "rad", "ax"),
            P("row", "rad", "ax"),
            P("row", "rad", "ax"),
            P(None, "rad"),
        ),
        out_specs=(P(None, "row", "rad", "ax", None), P(None, "row", "rad"), P("row", "rad")),
        check_vma=False,
    )
```

```python
import functools

import jax
import jax.numpy as jnp
from jax import lax
from jax.experimental import pallas as pl
from jax.experimental.pallas import tpu as pltpu
from jax.sharding import PartitionSpec as P

MESH = pl.DeviceIdType.MESH
SWEEPS = 4
NV = 7
PV = 4
SV = 3
RC = 8
CC = 8
NX = 128
BASE = (-1, -1, -1, -1, 1, 3, 2, 4, 4, 6, 6, 6, 7, 8, 10, 9)
DIRECT = 6
TX = 8


def kernel(
    sizes,
    state_h,
    speed_h,
    visc_h,
    relax_h,
    area_h,
    station_h,
    flags_h,
    inlet_h,
    out,
    out_profile,
    out_pressure,
    field,
    axs,
    axr,
    radr,
    ms_src,
    ms_own,
    ms_up,
    t_src,
    px,
    coef,
    weight,
    hot,
    upstream,
    inlet_t,
    ghosts,
    profile_s,
    tm_src,
    tm_own,
    tr,
    nb_src,
    nb_in,
    s_ax,
    r_ax,
    s_rad,
    r_rad,
    s_own,
    r_own,
    s_down,
    r_up,
    s_px,
    r_px,
    s_tm,
    r_tm,
    s_tr,
    r_tr,
    s_nb,
    r_nb,
    ready,
    state,
    speed,
    visc,
    relax,
    area,
    station,
    flags,
    inlet,
    s_in,
):
    rows, rads, axes = sizes
    row, rad, ax = lax.axis_index("row"), lax.axis_index("rad"), lax.axis_index("ax")
    lane = lax.broadcasted_iota(jnp.int32, (8, NX), 1)
    sub = lax.broadcasted_iota(jnp.int32, (8, NX), 0)
    zero = jnp.zeros((8, NX), jnp.float32)

    def remote(src, dst, ssem, rsem, where):
        return pltpu.make_async_remote_copy(
            src_ref=src, dst_ref=dst, send_sem=ssem, recv_sem=rsem, device_id=where, device_id_type=MESH
        )

    barrier = pltpu.get_barrier_semaphore()

    def greet(where):
        pl.semaphore_signal(barrier, inc=1, device_id=where, device_id_type=MESH)

    for d in range(1, axes):
        greet({"ax": lax.rem(ax + d, axes)})

    heard = [[r for r in range(BASE[x] + 1, x)] for x in range(rads)]
    own_pairs = [(r, x) for x in range(rads) for r in heard[x] if r < x - 1]
    sum_pairs = [(BASE[x], x) for x in range(rads) if BASE[x] >= 0]

    def table(values):
        out = jnp.int32(0)
        for i, value in enumerate(values):
            if value:
                out = out + jnp.where(rad == i, value, 0)
        return out

    def among(which):
        mask = sum(1 << r for r in which)
        return (lax.shift_right_logical(jnp.int32(mask), rad) & 1) == 1

    def distances(pairs):
        return [(d, [r for r, x in pairs if x - r == d]) for d in sorted({x - r for r, x in pairs}, reverse=True)]

    around = [lax.rem(ax + axes - 1, axes), ax, lax.rem(ax + 1, axes)]

    @pl.when(rad > 0)
    def _():
        for where in around:
            greet({"rad": rad - 1, "ax": where})

    @pl.when(rad < rads - 1)
    def _():
        for where in around:
            greet({"rad": rad + 1, "ax": where})

    for d, senders in distances(own_pairs + sum_pairs):

        @pl.when(among(senders))
        def _():
            greet({"rad": rad + d})

    @pl.when(row > 0)
    def _():
        for d in range(axes):
            greet({"row": row - 1, "ax": d})

    first_part, second_part = [
        [pltpu.make_async_copy(src, dst, s_in.at[k, i]) for i, (src, dst) in enumerate(pairs)]
        for k, pairs in enumerate(
            (
                (
                    (state_h.at[pl.ds(SV, 2)], state.at[pl.ds(SV, 2)]),
                    (speed_h, speed),
                    (visc_h, visc),
                    (area_h, area),
                    (station_h, station),
                    (flags_h, flags),
                ),
                (
                    (relax_h, relax),
                    (inlet_h, inlet),
                    (state_h.at[pl.ds(0, SV)], state.at[pl.ds(0, SV)]),
                    (state_h.at[pl.ds(PV + 1, NV - PV - 1)], state.at[pl.ds(PV + 1, NV - PV - 1)]),
                ),
            )
        )
    ]
    for load in first_part + second_part:
        load.start()

    @pl.when(rad == 0)
    def _():
        radr[:, 0] = jnp.zeros_like(radr[:, 0])
        tr[:, 0] = jnp.zeros_like(tr[:, 0])
        nb_in[0] = jnp.zeros_like(nb_in[0])

    @pl.when(rad == rads - 1)
    def _():
        radr[:, 1] = jnp.zeros_like(radr[:, 1])
        tr[:, 1] = jnp.zeros_like(tr[:, 1])
        nb_in[2] = jnp.zeros_like(nb_in[2])

    for d in range(1, DIRECT + 1):

        @pl.when(jnp.logical_not(among([x for x in range(rads) if x - d in heard[x]])))
        def _():
            px[d - 1] = jnp.zeros_like(px[d - 1])

    @pl.when(among([x for x in range(rads) if BASE[x] < 0]))
    def _():
        px[DIRECT] = jnp.zeros_like(px[DIRECT])

    diagonal = sub == lane

    def column(ref, r):
        wide = jnp.broadcast_to(ref[r : r + 1, :], (8, 8))
        return jnp.broadcast_to(jnp.sum(jnp.where(diagonal[:, :8], wide, 0.0), axis=1, keepdims=True), (8, NX))

    partners = sorted(range(1, axes), key=lambda d: (-min(d, axes - d), d))

    def greeted():
        fixed = [0] * rads
        for _, x in own_pairs + sum_pairs:
            fixed[x] += 1
        for x in range(rads):
            fixed[x] += 3 * (x > 0) + 3 * (x < rads - 1)
        pl.semaphore_wait(barrier, (axes - 1) + table(fixed) + jnp.where(row < rows - 1, axes, 0))
        for which, pairs in enumerate((own_pairs, sum_pairs)):
            for d, senders in distances(pairs):

                @pl.when(among([r + d for r in senders]))
                def _():
                    pl.semaphore_signal(ready.at[which], inc=1, device_id={"rad": rad - d}, device_id_type=MESH)

    def await_ready(which):
        counts = [0] * rads
        for r, _ in (own_pairs, sum_pairs)[which]:
            counts[r] += 1

        @pl.when(among([r for r in range(rads) if counts[r]]))
        def _():
            pl.semaphore_wait(ready.at[which], table(counts))

    last = SWEEPS

    group = lane // TX
    spot = lax.rem(lane, TX)
    middle = (group >= 4) & (group < 12)

    def doubled(x):
        return jnp.where(middle, x, pltpu.roll(x, 64, 1))

    def tail_pack(row_of):
        acc = zero
        for r in range(RC):
            acc = jnp.where(group == r + 4, pltpu.roll(row_of(r), (TX * (r + 5)) % NX, 1), acc)
        return doubled(acc)

    def wide(p):
        return 2 * RC if p in (2, 3) else RC

    def tail_copy(p, d):
        n = wide(p)
        return remote(
            tm_src.at[p, pl.ds(0, n)],
            tm_own.at[p, ax, pl.ds(0, n)],
            s_tm.at[p],
            r_tm.at[p],
            {"ax": lax.rem(ax + d, axes)},
        )

    def tail_all(p):
        part = tm_own.at[p, pl.ds(0, axes - 1), pl.ds(0, wide(p))]
        return remote(part, part, s_tm.at[p], r_tm.at[p], {"ax": ax})

    def tail_rad(p, up):
        side = 0 if up else 1
        where = {"rad": rad + 1 if up else rad - 1}
        return remote(
            tm_src.at[p, pl.ds(RC, RC)], tr.at[p, side], s_tr.at[p, side], r_tr.at[p, side], where
        )

    def near_copy(i, j):
        n = 3 * i + j
        where = {"rad": rad + 1 - i, "ax": around[2 - j]}
        return remote(nb_src, nb_in.at[i, j], s_nb.at[n], r_nb.at[n], where)

    def near_each(action, sent):
        for j in (0, 2, 1):
            for i in (0, 2, 1):
                if i == 1 and j == 1:
                    continue
                if i == 1:
                    action(near_copy(i, j))
                elif (i == 0) == sent:

                    @pl.when(rad < rads - 1)
                    def _():
                        action(near_copy(i, j))

                else:

                    @pl.when(rad > 0)
                    def _():
                        action(near_copy(i, j))

    def total_copy(k, d):
        part = pl.ds(0, 1) if k == 0 else pl.ds(1, SWEEPS - 1)
        return remote(t_src.at[0, part], px.at[d - 1, part], s_px.at[k, d - 1], r_px.at[k, d - 1], {"rad": rad + d})

    def sum_copy(k, d):
        where = {"rad": rad + d}
        part = pl.ds(0, 1) if k == 0 else pl.ds(1, SWEEPS - 1)
        return remote(t_src.at[1, part], px.at[DIRECT, part], s_px.at[k, DIRECT + d - 1], r_px.at[k, DIRECT], where)

    own_steps = distances(own_pairs + [(x - 1, x) for x in range(1, rads)])
    sum_steps = distances(sum_pairs)

    for load in first_part:
        load.wait()
    areas = area[...]
    local_station = (station[...] - rad * RC).astype(jnp.float32)
    tail_station = zero
    tail_area = zero
    for r in range(RC):
        st = column(local_station, r)
        ar = column(areas, r)
        hot[r] = st
        for s in range(RC):
            weight[s, r] = jnp.where(st == float(s), ar, 0.0)
        mine = group == r + 4
        tail_station = jnp.where(mine, st, tail_station)
        tail_area = jnp.where(mine & (spot >= TX - 3), ar, tail_area)

    def tail_sums(last_one, middle_one, first_one):
        q = jnp.where(spot == TX - 1, last_one, zero)
        q = jnp.where(spot == TX - 2, middle_one, q)
        q = jnp.where(spot == TX - 3, first_one, q)
        total = zero
        for s in range(RC):
            part = jnp.sum(jnp.where(tail_station == float(s), tail_area, 0.0) * q, axis=0, keepdims=True)
            total = jnp.where(sub == s, part, total)
        return total

    def back(x, by):
        return pltpu.roll(x, NX - by, 1)

    def tail_send(p, total):
        tm_src[p, 0:RC] = total
        tm_own[p, ax, 0:RC] = total
        for d in partners:
            tail_copy(p, d).start()
        if wide(p) > RC:

            @pl.when(rad > 0)
            def _():
                tail_rad(p, False).start()

            @pl.when(rad < rads - 1)
            def _():
                tail_rad(p, True).start()

        if p == last:

            @pl.when(row < rows - 1)
            def _():
                for d in partners + [0]:
                    up_copy(p, d).start()

    def up_copy(p, d):
        src = tm_src.at[p, pl.ds(0, RC)] if p == last else ms_src.at[p]
        return remote(src, ms_up.at[p, ax], s_down.at[p], r_up.at[p], {"row": row + 1, "ax": lax.rem(ax + d, axes)})

    def fold(total):
        for step in (8, 16, 32):
            total = total + pltpu.roll(total, step, 1)
        return total

    def at(x, i):
        return jnp.broadcast_to(x[:, i : i + 1], (8, NX))

    flag = flags[...].astype(jnp.float32)
    tail_flag = zero
    for r in range(RC):
        fl = 0.5 * column(flag, r)
        tail_flag = jnp.where(group == r + 4, fl, tail_flag)
        a = 0.5 * speed[r]
        coef[0, r] = a
        coef[1, r] = a * fl
        coef[2, r] = 0.5 * visc[r]
    tails = [
        tail_pack(lambda r: state[SV, r]),
        tail_pack(lambda r: state[PV, r]),
        tail_pack(lambda r: coef[0, r]),
        tail_pack(lambda r: coef[2, r]),
        doubled(tail_flag),
    ]
    for i, x in enumerate(tails):
        nb_src[i] = x
    greeted()
    tail_send(0, tail_sums(tails[0], 1.0, back(tails[1], 2)))
    near_each(lambda copy: copy.start(), True)
    tail = tails[1]

    def sums(picks, p):
        total = zero
        for s in range(RC):
            acc = weight[s, 0] * picks[0]
            for r in range(1, RC):
                acc = acc + weight[s, r] * picks[r]
            total = jnp.where(sub == s, jnp.sum(acc, axis=0, keepdims=True), total)
        ms_src[p] = total
        if p == last - 1:
            ms_own[ax] = total

    def pack(src, p, v):
        for r in range(RC):
            axs[p, 0, v, r : r + 1, :] = src[v, r, 0:1, :]
            axs[p, 1, v, r : r + 1, :] = src[v, r, CC - 1 : CC, :]

    def of(p):
        return state if p == 0 else field.at[p - 1]

    def rad_copy(p, up):
        src = of(p)
        edge = RC - 1 if up else 0
        where = {"rad": rad + 1 if up else rad - 1}
        side = 0 if up else 1
        if p == last:
            return remote(src.at[PV, edge], radr.at[p, side, PV], s_rad.at[p, side], r_rad.at[p, side], where)
        return remote(src.at[:, edge], radr.at[p, side], s_rad.at[p, side], r_rad.at[p, side], where)

    def ax_copy(p, up):
        cell = 1 if up else 0
        where = {"ax": lax.rem(ax + (1 if up else axes - 1), axes)}
        side = 0 if up else 1
        if p == last:
            return remote(axs.at[p, cell, PV], axr.at[p, side, PV], s_ax.at[p, side], r_ax.at[p, side], where)
        return remote(axs.at[p, cell], axr.at[p, side], s_ax.at[p, side], r_ax.at[p, side], where)

    def own_copy(d):
        return remote(ms_src.at[last - 1], ms_own.at[ax], s_own, r_own, {"ax": lax.rem(ax + d, axes)})

    def field_send(p):
        if p < last:

            @pl.when(row < rows - 1)
            def _():
                for d in partners + [0]:
                    up_copy(p, d).start()

        @pl.when(rad < rads - 1)
        def _():
            rad_copy(p, True).start()

        @pl.when(rad > 0)
        def _():
            rad_copy(p, False).start()

        ax_copy(p, True).start()
        ax_copy(p, False).start()
        if p == last - 1:
            for d in partners:
                own_copy(d).start()

    def update(q, rm, rp, left, right, coefs, ghost, edge, keep):
        a, ah, nu = coefs
        qm = jnp.where(lane == 0, ghost, pltpu.roll(q, 1, 1))
        b = q - qm
        f = jnp.where(lane == NX - 1, edge, pltpu.roll(b, NX - 1, 1))
        slope = jnp.maximum(jnp.minimum(b, f), 0.0) + jnp.minimum(jnp.maximum(b, f), 0.0)
        g = a * q + ah * slope
        flux_in = jnp.where(lane == 0, a * ghost, pltpu.roll(g, 1, 1))
        cm = jnp.where(sub == 0, left, pltpu.roll(q, 1, 0))
        cp = jnp.where(sub == CC - 1, right, pltpu.roll(q, CC - 1, 0))
        lap = (f - b) + (rm + rp) + (cm + cp) - 4.0 * q
        return q * keep + (flux_in - g) + nu * lap

    def tail_step(q, lower, upper, cm, cp, coefs, keep, edge):
        a, ah, nu = coefs
        b = q - pltpu.roll(q, 1, 1)
        f = jnp.where(spot == TX - 1, edge, back(b, 1))
        slope = jnp.maximum(jnp.minimum(b, f), 0.0) + jnp.minimum(jnp.maximum(b, f), 0.0)
        g = a * q + ah * slope
        lap = (f - b) + (lower + upper) + (cm + cp) - 4.0 * q
        return q * keep + (pltpu.roll(g, 1, 1) - g) + nu * lap

    def tail_update(p, q, ghost):
        if p == 1:
            lo, hi, left, right = [nb_in[i, j, 1] for i, j in ((0, 1), (2, 1), (1, 0), (1, 2))]
        else:
            lo, hi = tr[p, 0], tr[p, 1]
            left, right = [tm_own[p, around[j], RC : 2 * RC] for j in (0, 2)]
        full = jnp.where(group < 4, lo, jnp.where(group < 12, q, hi))
        cm = jnp.where(sub == 0, left[CC - 1 : CC], pltpu.roll(q, 1, 0))
        cp = jnp.where(sub == CC - 1, right[0:1], pltpu.roll(q, CC - 1, 0))
        coefs = (tails[2], tails[2] * tails[4], tails[3])
        keep = 1.0 - 0.5 * relax[PV]
        new = tail_step(q, pltpu.roll(full, TX, 1), back(full, TX), cm, cp, coefs, keep, ghost - q)
        return doubled(new)

    def deep(i):
        def comb(j):
            own = tails[i] if j == 1 else nb_in[1, j, i]
            return jnp.where(group < 4, nb_in[0, j, i], jnp.where(group < 12, own, nb_in[2, j, i]))

        return comb(1), jnp.where(sub < 4, comb(2), comb(0))

    def deep_sections():
        pair = deep(0)
        a, nu, fl = deep(2), deep(3), deep(4)
        keep = 1.0 - 0.5 * relax[SV]
        found = []
        for _ in range(SWEEPS - 1):
            new = []
            for h in range(2):
                q, other = pair[h], pair[1 - h]
                cm = jnp.where(sub == 0, other[CC - 1 : CC], pltpu.roll(q, 1, 0))
                cp = jnp.where(sub == CC - 1, other[0:1], pltpu.roll(q, CC - 1, 0))
                coefs = (a[h], a[h] * fl[h], nu[h])
                new.append(tail_step(q, pltpu.roll(q, TX, 1), back(q, TX), cm, cp, coefs, keep, 0.0))
            pair = new
            found.append(pair[0])
        return found

    def sweep(p, v, src, dst, pressures):
        keep = 1.0 - 0.5 * relax[v]
        fresh = []
        for r in range(RC):
            q = src[v, r]
            rm = radr[p, 0, v] if r == 0 else src[v, r - 1]
            rp = radr[p, 1, v] if r == RC - 1 else src[v, r + 1]
            left = axr[p, 0, v, r : r + 1, :]
            right = axr[p, 1, v, r : r + 1, :]
            ghost = pltpu.roll(ghosts[r], (NX - v) % NX if isinstance(v, int) else lax.rem(NX - v, NX), 1)
            edge = 0.0 if pressures is None else pressures[r] - q
            new = update(q, rm, rp, left, right, (coef[0, r], coef[1, r], coef[2, r]), ghost, edge, keep)
            dst[v, r] = new
            fresh.append(new)
        return fresh

    for load in second_part:
        load.wait()
    one = jnp.where(lane == NV, 1.0, 0.0)

    def first(v, picks):
        pack(state, 0, v)
        return tuple(jnp.where(lane == v, at(state[v, r], NX - 1), picks[r]) for r in range(RC))

    sums(lax.fori_loop(0, NV, first, (one,) * RC), 0)
    field_send(0)

    for r in range(RC):
        field[0, PV, r] = state[PV, r]
    turned = zero
    inlet_all = inlet[...]
    for v in range(NV):
        turned = jnp.where(lane == v, column(inlet_all, v), turned)
    inlet_t[...] = turned
    radius = 1.0 + (rad * RC + sub).astype(jnp.float32) / float(RC * rads)

    def write_profile(v, wide):
        line = jnp.sum(jnp.where(diagonal, wide, 0.0), axis=0, keepdims=True)
        out_profile[v] = line[:, :RC]

    def total_of(load):
        total = load(0)
        for d in range(1, axes):
            total = total + load(d)
        return total

    def send_totals(k):
        for d, senders in own_steps:

            @pl.when(among(senders))
            def _():
                total_copy(k, d).start()

    def totals_in(k):
        for d, senders in own_steps:

            @pl.when(among([r + d for r in senders]))
            def _():
                total_copy(k, d).wait_recv()

        @pl.when(among([x for x in range(rads) if BASE[x] >= 0]))
        def _():
            sum_copy(k, 1).wait_recv()

        before = []
        for i in range(1) if k == 0 else range(1, SWEEPS):
            before.append(jnp.sum(px[:, i], axis=0))
            t_src[1, i] = before[-1] + t_src[0, i]
        if k == 0:
            await_ready(1)
        for d, senders in sum_steps:

            @pl.when(among(senders))
            def _():
                sum_copy(k, d).start()

        return before

    scale = 4.0 / (RC * rads)
    swirls, befores = [], []

    def add_swirl(third):
        swirls.append(third * third / radius)
        t_src[0, len(swirls) - 1] = jnp.sum(swirls[-1], axis=0, keepdims=True)

    def sent(p):
        tail_all(p).wait_send()

        @pl.when(row < rows - 1)
        def _():
            remote(ms_up.at[p], ms_up.at[p], s_down.at[p], r_up.at[p], {"ax": ax}).wait_send()

        @pl.when(rad < rads - 1)
        def _():
            rad_copy(p, True).wait_send()
            if wide(p) > RC:
                tail_rad(p, True).wait_send()

        @pl.when(rad > 0)
        def _():
            rad_copy(p, False).wait_send()
            if wide(p) > RC:
                tail_rad(p, False).wait_send()

        ax_copy(p, True).wait_send()
        ax_copy(p, False).wait_send()

    def totals_sent(k):
        for d, senders in own_steps:

            @pl.when(among(senders))
            def _():
                total_copy(k, d).wait_send()

        for d, senders in sum_steps:

            @pl.when(among(senders))
            def _():
                sum_copy(k, d).wait_send()

    own_part = ms_own.at[pl.ds(0, axes - 1)]
    own_all = remote(own_part, own_part, s_own, r_own, {"ax": ax})

    for p in range(SWEEPS + 1):
        if p == last:
            own_all.wait_recv()
            total = total_of(lambda d: ms_own[d])
            profile = total / at(total, NV)
            for v in range(NV):
                if v != PV:
                    write_profile(v, at(profile, v))
            own_all.wait_send()
            sent(p - 1)

        tail_all(p).wait_recv()
        folded = fold(total_of(lambda d: tm_own[p, d, 0:RC]))
        if p == 0:
            areas_in = at(folded, 94)
            fourth = at(folded, 93) / areas_in
            add_swirl(at(folded, 95) / areas_in)
            await_ready(0)
            send_totals(0)
            near_each(lambda copy: copy.wait_recv(), False)
            one_on, two_on, three_on = deep_sections()
            tail_send(1, tail_sums(one_on, back(two_on, 1), back(three_on, 2)))
        else:
            if p == 1:
                for i in (95, 94, 93):
                    add_swirl(at(folded, i) / areas_in)
                send_totals(1)
            else:
                fourth = at(folded, 95) / areas_in
            if wide(p) > RC:

                @pl.when(rad > 0)
                def _():
                    tail_rad(p, True).wait_recv()

                @pl.when(rad < rads - 1)
                def _():
                    tail_rad(p, False).wait_recv()

            run = swirls[p - 1]
            for step in (1, 2, 4):
                run = run + jnp.where(sub >= step, pltpu.roll(run, step, 0), 0.0)
            pressure = fourth + scale * ((run - swirls[p - 1]) + befores[p - 1])
            profile_s[...] = pressure
            rows_of = [profile_s[s : s + 1, :] for s in range(RC)]
            if p < last:
                ghost = jnp.broadcast_to(rows_of[0], (8, NX))
                for s in range(1, RC):
                    ghost = jnp.where(tail_station == float(s), rows_of[s], ghost)
                tail = tail_update(p, tail, ghost)
                if wide(p + 1) > RC:
                    tm_src[p + 1, RC:] = tail
                tail_send(p + 1, tail_sums(tail, 1.0, zero))

        src = of(p)

        @pl.when(row == 0)
        def _():
            upstream[...] = inlet_t[...]

        @pl.when(row > 0)
        def _():
            remote(ms_up.at[p], ms_up.at[p], s_down.at[p], r_up.at[p], {"ax": ax}).wait_recv()
            total = total_of(lambda d: ms_up[p, d])
            if p == last:
                total = fold(total)
                upstream[...] = at(total, 95) / at(total, 94)
            else:
                upstream[...] = total / at(total, NV)

        for r in range(RC):
            st = hot[r]
            acc = jnp.broadcast_to(upstream[0:1, :], (8, NX))
            for s in range(1, RC):
                acc = jnp.where(st == float(s), upstream[s : s + 1, :], acc)
            ghosts[r] = acc

        @pl.when(rad > 0)
        def _():
            rad_copy(p, True).wait_recv()

        @pl.when(rad < rads - 1)
        def _():
            rad_copy(p, False).wait_recv()

        ax_copy(p, True).wait_recv()
        ax_copy(p, False).wait_recv()

        dst = field.at[p] if p + 1 < SWEEPS else out
        picks = (one,) * RC
        if p < SWEEPS:

            def plain(i, picks):
                v = i + (1 if i >= PV else 0)
                fresh = sweep(p, v, src, dst, None)
                if p + 1 == SWEEPS:
                    return picks
                pack(dst, p + 1, v)
                return tuple(jnp.where(lane == v, at(fresh[r], NX - 1), picks[r]) for r in range(RC))

            for i in range(NV - 1):
                picks = plain(i, picks)
        if p > 0:
            pressures = []
            for r in range(RC):
                st = hot[r]
                acc = jnp.broadcast_to(rows_of[0], (8, NX))
                for s in range(1, RC):
                    acc = jnp.where(st == float(s), rows_of[s], acc)
                pressures.append(acc)
            fresh = sweep(p, PV, src, field.at[p] if p < SWEEPS else out, pressures)
        else:
            fresh = [state[PV, r] for r in range(RC)]
        if p < SWEEPS:
            pack(field.at[p], p + 1, PV)
            if p + 1 < SWEEPS:
                sums(tuple(jnp.where(lane == PV, at(fresh[r], NX - 1), picks[r]) for r in range(RC)), p + 1)
            field_send(p + 1)
        if p == 0:
            befores += totals_in(0)
        if p == 1:
            befores += totals_in(1)
            near_each(lambda copy: copy.wait_send(), True)
        if 1 <= p < last:
            sent(p - 1)
        if p == 2:
            totals_sent(0)
        if p == 3:
            totals_sent(1)

    write_profile(PV, fourth)
    out_pressure[...] = jnp.sum(jnp.where(diagonal, pressure, 0.0), axis=0, keepdims=True)[:, :RC]
    sent(last)


def store(new, profile, pressure, out, out_profile, out_pressure, sems):
    copies = [
        pltpu.make_async_copy(src, dst, sems.at[i])
        for i, (src, dst) in enumerate(((new, out), (profile, out_profile), (pressure, out_pressure)))
    ]
    for copy in copies:
        copy.start()
    for copy in copies:
        copy.wait()


def solution(mesh):
    sizes = (mesh.shape["row"], mesh.shape["rad"], mesh.shape["ax"])
    axes = sizes[2]
    phases = SWEEPS + 1

    def body(state, speed, visc, relax, area, station, flags, inlet):
        vmem = pl.BlockSpec(memory_space=pltpu.VMEM)
        hbm = pl.BlockSpec(memory_space=pltpu.HBM)
        f32 = jnp.float32
        dma = pltpu.SemaphoreType.DMA
        new, profile, pressure = pl.pallas_call(
            functools.partial(kernel, sizes),
            out_shape=(
                jax.ShapeDtypeStruct((NV, RC, CC, NX), f32),
                jax.ShapeDtypeStruct((NV, 1, RC), f32),
                jax.ShapeDtypeStruct((1, RC), f32),
            ),
            in_specs=[hbm] * 8,
            out_specs=(vmem, vmem, vmem),
            scratch_shapes=[
                pltpu.VMEM((SWEEPS, NV, RC, CC, NX), f32),
                pltpu.VMEM((phases, 2, NV, RC, NX), f32),
                pltpu.VMEM((phases, 2, NV, RC, NX), f32),
                pltpu.VMEM((phases, 2, NV, CC, NX), f32),
                pltpu.VMEM((phases, RC, NX), f32),
                pltpu.VMEM((axes, RC, NX), f32),
                pltpu.VMEM((phases, axes, RC, NX), f32),
                pltpu.VMEM((2, SWEEPS, 1, NX), f32),
                pltpu.VMEM((DIRECT + 1, SWEEPS, 1, NX), f32),
                pltpu.VMEM((3, RC, CC, NX), f32),
                pltpu.VMEM((RC, RC, CC, NX), f32),
                pltpu.VMEM((RC, CC, NX), f32),
                pltpu.VMEM((RC, NX), f32),
                pltpu.VMEM((RC, NX), f32),
                pltpu.VMEM((RC, CC, NX), f32),
                pltpu.VMEM((RC, NX), f32),
                pltpu.VMEM((phases, 2 * RC, NX), f32),
                pltpu.VMEM((phases, axes, 2 * RC, NX), f32),
                pltpu.VMEM((SWEEPS, 2, CC, NX), f32),
                pltpu.VMEM((5, CC, NX), f32),
                pltpu.VMEM((3, 3, 5, CC, NX), f32),
                dma((phases, 2)),
                dma((phases, 2)),
                dma((phases, 2)),
                dma((phases, 2)),
                dma,
                dma,
                dma((phases,)),
                dma((phases,)),
                dma((2, 2 * DIRECT + 1)),
                dma((2, DIRECT + 1)),
                dma((phases,)),
                dma((phases,)),
                dma((SWEEPS, 2)),
                dma((SWEEPS, 2)),
                dma((9,)),
                dma((9,)),
                pltpu.SemaphoreType.REGULAR((2,)),
                pltpu.VMEM((NV, RC, CC, NX), f32),
                pltpu.VMEM((RC, CC, NX), f32),
                pltpu.VMEM((RC, CC, NX), f32),
                pltpu.SMEM((NV,), f32),
                pltpu.VMEM((RC, CC), f32),
                pltpu.VMEM((RC, CC), jnp.int32),
                pltpu.VMEM((RC, CC), jnp.int32),
                pltpu.VMEM((NV, RC), f32),
                dma((2, 8)),
            ],
            compiler_params=pltpu.CompilerParams(
                collective_id=0, has_side_effects=True, vmem_limit_bytes=16 * 1024 * 1024
            ),
        )(
            *[
                pltpu.with_memory_space_constraint(x, pltpu.HBM)
                for x in (
                    state.reshape(NV, RC, CC, NX),
                    speed.reshape(RC, CC, NX),
                    visc.reshape(RC, CC, NX),
                    relax,
                    area.reshape(RC, CC),
                    station.reshape(RC, CC),
                    flags.reshape(RC, CC),
                    inlet,
                )
            ]
        )
        new, profile, pressure = pl.pallas_call(
            store,
            out_shape=(
                jax.ShapeDtypeStruct((NV, RC, CC, NX), f32),
                jax.ShapeDtypeStruct((NV, 1, RC), f32),
                jax.ShapeDtypeStruct((1, RC), f32),
            ),
            in_specs=[vmem] * 3,
            out_specs=(hbm,) * 3,
            scratch_shapes=[dma((3,))],
            compiler_params=pltpu.CompilerParams(vmem_limit_bytes=4 * 1024 * 1024),
        )(new, profile, pressure)
        return new[:, None], profile, pressure

    return jax.shard_map(
        body,
        mesh=mesh,
        in_specs=(
            P(None, "row", "rad", "ax", None),
            P("row", "rad", "ax", None),
            P("row", "rad", "ax", None),
            P(),
            P("row", "rad", "ax"),
            P("row", "rad", "ax"),
            P("row", "rad", "ax"),
            P(None, "rad"),
        ),
        out_specs=(P(None, "row", "rad", "ax", None), P(None, "row", "rad"), P("row", "rad")),
        check_vma=False,
    )
```
